128 devices in a mesh: gx: 8 (over x, core), gy: 16 (over y, z).
Axes of the slice: x: 4, y: 4, z: 4, core: 2. Of those that a mesh axis runs over, the one named last changes fastest.
Arguments:
- fluxes: float32 [6, 16, 81920], P(None, None, ('gx', 'gy')), may hold values from -6 to 6
- remap_weights: float32 [32, 16, 32768], P(None, None, ('gx', 'gy')), may hold values from 0 to 0.25
- source_elem: int32 [32768], P(('gx', 'gy')), may hold values from 0 to 639
- owner_map: int32 [32, 32768], P(None, ('gx', 'gy')), may hold values from 0 to 127, as said below
- target_cell: int32 [32, 32768], P(None, ('gx', 'gy')), may hold values from 0 to 16383
- ocean_state: float32 [4, 8, 512, 4096], P(None, None, 'gx', 'gy'), may hold values from -6 to 6
- wet_mask: int32 [512, 4096], P('gx', 'gy'), may hold values 0 or 1
Outputs:
- new_state: float32 [4, 8, 512, 4096], P(None, None, 'gx', 'gy')
The draws below stay inside these ranges and needn't reach their ends.
Inputs may be any that keep to these rules, and one draw needn't show every extreme that they name: `owner_map`: among the rows of one device no owner is named more than 256 times; one owner, the same for every device, is named exactly 256 times by every device.
All inputs are finite; a program needn't handle non-finite values. No bound on the sum of `wet_mask` on one device may be relied on, other than what follows from the above.
Results may differ from the reference program's by a relative error of at most 0.0003.
Values sent between devices are 32-bit elements; how exact they have to be, the bound alone decides.
No kernel may reach another device: no remote copies, remote signals or barrier semaphores. Data moves between devices by JAX's collectives and lax.ppermute only.
A program may use at most 64 MiB of HBM per device.

```python
import jax
import jax.numpy as jnp
from jax import lax

NF = 6
NP2 = 16
BT = 32
L = 8
STEPS = 4
AEL_DEV = 640
NBLK_DEV = 256
CX = 64
CY = 256
AELEM = 81920
NBLK = 32768
R_DEV = 8192
CAP = 256
OC_DEV = 16384
NXO = 512
NYO = 4096
N_GY = 16
DEVICES = 128


def draw_owner_map(key, part):
    key = jax.random.fold_in(key, 7)
    hot_key, shift_key, shuffle_key = jax.random.split(key, 3)
    hottest = jax.random.randint(hot_key, (), 0, DEVICES)
    shifts = jax.random.randint(shift_key, (DEVICES, 1), 0, DEVICES - 1)
    row_index = jnp.arange(R_DEV, dtype=jnp.int32)[None, :]
    others = (hottest + 1 + (row_index - CAP + shifts) % (DEVICES - 1)) % DEVICES
    plan = jnp.where(row_index < CAP, hottest, others)
    shuffles = jax.vmap(lambda sub: jax.random.permutation(sub, R_DEV))(jax.random.split(shuffle_key, DEVICES))
    mixed = jnp.take_along_axis(plan, shuffles, axis=1)
    mixed = mixed.reshape(DEVICES, BT, NBLK_DEV).transpose(1, 0, 2).reshape(BT, DEVICES * NBLK_DEV)
    return mixed.astype(jnp.int32)


def set_ends(values, rng, smallest, high):
    extent = values.shape
    place = [jax.random.randint(jax.random.fold_in(rng, axis), (), 0, extent[axis]) for axis in range(len(extent))]
    values = values.at[tuple(place)].set(smallest)
    longest = extent.index(max(extent))
    place[longest] = (place[longest] + 1) % extent[longest]
    return values.at[tuple(place)].set(high)


def block_scale(key, dims, shards, low, high):
    level = 1.0
    for axis_at, parts in shards:
        heights = jax.random.uniform(jax.random.fold_in(jax.random.fold_in(key, 6), axis_at), (parts,), jnp.float32, low / len(shards), high / len(shards))
        level = level * jnp.repeat(jnp.exp(heights), dims[axis_at] // parts).reshape((-1,) + (1,) * (len(dims) - 1 - axis_at))
    return level


def scatter_about(stream_key, extent, width, most, shards=(), kind=jnp.bfloat16):
    loudness = block_scale(stream_key, extent, shards, -0.22, 0.18) if shards else 1.0
    values = jax.random.normal(stream_key, extent, jnp.float32) * width * loudness
    return jnp.minimum(jnp.maximum(values, -most), most).astype(kind)


def setup_inputs(seed: int = 0) -> dict:
    splits = jax.random.split(jax.random.key(seed), 8)
    return {
        "fluxes": scatter_about(splits[0], (NF, NP2, AELEM), 1.0, 6.0, ((2, 128),), jnp.float32),
        "remap_weights": jnp.clip(0.25 * jax.random.uniform(splits[1], (BT, NP2, NBLK), jnp.float32) ** block_scale(splits[1], (BT, NP2, NBLK), ((2, 128),), -0.2, 0.2), 0.0, 0.25),
        "source_elem": set_ends(jax.random.randint(splits[2], (NBLK,), 0, AEL_DEV), jax.random.fold_in(splits[2], 1), 0, AEL_DEV - 1).astype(jnp.int32),
        "owner_map": draw_owner_map(jax.random.fold_in(splits[7], 71), 0),
        "target_cell": set_ends(jax.random.randint(splits[4], (BT, NBLK), 0, OC_DEV), jax.random.fold_in(splits[4], 1), 0, OC_DEV - 1).astype(jnp.int32),
        "ocean_state": scatter_about(splits[5], (4, L, NXO, NYO), 1.0, 6.0, ((2, 8), (3, 16)), jnp.float32),
        "wet_mask": set_ends((jax.random.randint(splits[6], (NXO, NYO), 0, 5) < 4).astype(jnp.int32), jax.random.fold_in(splits[6], 1), 0, 1),
    }


TIME_STEP = 0.1
VISCOSITY = 0.25
THERMAL_EXP = 0.2
HALINE_CONTR = 0.2
LAYER_THICK = 1.0
MIX_BASE = 0.3
MIX_WIND = 1.2
SOLAR_GAIN = 0.5
CORIOLIS_MID = 0.5
CORIOLIS_BETA = 0.5


def substep(padded, wet_cells, forcing, coriolis):
    center = padded[:, :, 1:-1, 1:-1]
    east_side = padded[:, :, 2:, 1:-1]
    west_side = padded[:, :, :-2, 1:-1]
    north_side = padded[:, :, 1:-1, 2:]
    south_side = padded[:, :, 1:-1, :-2]
    laplace = east_side + west_side + north_side + south_side - 4.0 * center
    slope_x = 0.5 * (east_side - west_side)
    slope_y = 0.5 * (north_side - south_side)
    zonal_flow = center[0]
    merid_flow = center[1]
    advect = zonal_flow * slope_x + merid_flow * slope_y
    density = HALINE_CONTR * padded[3] - THERMAL_EXP * padded[2]
    pressure = jnp.cumsum(density, axis=0) * LAYER_THICK
    grad_x = 0.5 * (pressure[:, 2:, 1:-1] - pressure[:, :-2, 1:-1])
    grad_y = 0.5 * (pressure[:, 1:-1, 2:] - pressure[:, 1:-1, :-2])
    mixing = forcing[5] * forcing[5]
    mixing = mixing / (1.0 + mixing)
    levels = jnp.arange(center.shape[1], dtype=jnp.float32)
    diffusivity = MIX_BASE + MIX_WIND * jnp.exp(-levels[:-1])[:, None, None] * mixing[None]
    interface = diffusivity[None] * (center[:, 1:] - center[:, :-1])
    no_flux = jnp.zeros_like(center[:, :1])
    vertical = jnp.concatenate([interface, no_flux], axis=1) - jnp.concatenate([no_flux, interface], axis=1)
    surface = jnp.where(levels == 0.0, 1.0, 0.0).astype(jnp.float32)[:, None, None]
    profile = (SOLAR_GAIN * jnp.exp(-0.5 * levels))[:, None, None]
    common = -advect + VISCOSITY * laplace + vertical
    tend_u = common[0] + coriolis * merid_flow - grad_x + surface * forcing[0]
    tend_v = common[1] - coriolis * zonal_flow - grad_y + surface * forcing[1]
    tend_t = common[2] + surface * forcing[2] + profile * forcing[3]
    tend_s = common[3] + surface * forcing[4]
    tendency = jnp.stack([tend_u, tend_v, tend_t, tend_s])
    return wet_cells * (center + TIME_STEP * tendency)


def coupled_forcing(fluxes, remap_weights, source_elem, owner_map, target_cell):
    device = jnp.arange(source_elem.shape[0], dtype=jnp.int32) // NBLK_DEV
    element = (device * AEL_DEV + source_elem).astype(jnp.int32)
    gathered = jnp.take(fluxes, element, axis=2)
    pieces = jnp.einsum("tsj,fsj->ftj", remap_weights, gathered, precision=lax.Precision.HIGHEST)
    grid_row = (owner_map // N_GY) * CX + target_cell // CY
    grid_col = (owner_map % N_GY) * CY + target_cell % CY
    flat_index = (grid_row * NYO + grid_col).reshape(-1).astype(jnp.int32)
    forcing = jnp.zeros((NF, NXO * NYO), jnp.float32).at[:, flat_index].add(pieces.reshape(NF, -1))
    return forcing.reshape(NF, NXO, NYO)


def reference(fluxes, remap_weights, source_elem, owner_map, target_cell, ocean_state, wet_mask):
    forcing = coupled_forcing(fluxes, remap_weights, source_elem, owner_map, target_cell)
    wet_cells = wet_mask.astype(jnp.float32)
    along_y = jnp.arange(NYO, dtype=jnp.float32)
    coriolis = jnp.broadcast_to(CORIOLIS_MID + CORIOLIS_BETA * (along_y / NYO - 0.5), (NXO, NYO))
    current = ocean_state * wet_cells
    for repeat in range(STEPS):
        padded = jnp.pad(current, ((0, 0), (0, 0), (1, 1), (1, 1)))
        current = substep(padded, wet_cells, forcing, coriolis)
    return current
```

```python
import math

import jax
import jax.numpy as jnp
from jax import lax
from jax.sharding import PartitionSpec as P
from jax.experimental import pallas as pl
from jax.experimental.pallas import tpu as pltpu
F32, BF16, I32 = jnp.float32, jnp.bfloat16, jnp.int32
FIELDS, LEVELS, HALO, STEPS = 4, 8, 4, 4
ROWS_DIMS = (((1,), (1,)), ((), ()))


def iota(shape, dim, dtype=I32):
    return lax.broadcasted_iota(dtype, shape, dim)


def split2(v):
    top = v.astype(BF16).astype(F32)
    return top, v - top


def pack_kernel(flux_ref, weight0_ref, weight1_ref, source_ref, owner_ref, cell_ref, out_ref,
                gathered0, gathered1, payload0, payload1, hots, place, sorted_rows, left, right, marks, marks_s, sem):
    nt, nj = owner_ref.shape
    owners = out_ref.shape[0]
    fields, nodes = 6, 16
    flux = flux_ref[...]
    f1 = flux.astype(BF16)
    r1 = flux - f1.astype(F32)
    f2 = r1.astype(BF16)
    f3 = (r1 - f2.astype(F32)).astype(BF16)
    elem_hot = jnp.where(iota((flux.shape[1], nj), 0) == source_ref[...], 1.0, 0.0).astype(BF16)
    g = jnp.dot(f1, elem_hot, preferred_element_type=F32)
    g = g + jnp.dot(f2, elem_hot, preferred_element_type=F32)
    g = g + jnp.dot(f3, elem_hot, preferred_element_type=F32)
    gathered0[...] = g[:, :128]
    gathered1[...] = g[:, 128:]
    halves = ((weight0_ref, gathered0, payload0), (weight1_ref, gathered1, payload1))
    for half, (weight_ref, gathered, payload) in enumerate(halves):
        for f in range(fields):
            acc = None
            for s in range(nodes):
                term = weight_ref[pl.ds(s, nt, stride=nodes), :] * gathered[pl.ds(f * nodes + s, 1), :]
                acc = term if acc is None else acc + term
            payload[pl.ds(f, nt, stride=8), :] = acc
        payload[pl.ds(6, nt, stride=8), :] = cell_ref[:, pl.ds(half * 128, 128)].astype(F32)
        payload[pl.ds(7, nt, stride=8), :] = jnp.zeros((nt, 128), F32)
    owner_iota = iota((owners, nj), 0)
    total = None
    for t in range(nt):
        hot = jnp.where(owner_iota == owner_ref[pl.ds(t, 1), :], 1.0, 0.0).astype(BF16)
        hots[pl.ds(t * owners, owners), :] = hot
        total = hot if total is None else total + hot
    ones = jnp.ones((nj, owners), BF16)
    tot_col = jnp.dot(total, ones, preferred_element_type=F32)
    tot_row = lax.dot_general(jnp.ones((8, nj), BF16), total, ROWS_DIMS, preferred_element_type=F32)
    a = iota((owners, owners), 0)
    b = iota((owners, owners), 1)
    before = jnp.where(b < a, 1.0, 0.0).astype(BF16)
    after = jnp.where(a < b, 1.0, 0.0).astype(BF16)
    base = jnp.dot(before, tot_col.astype(BF16), preferred_element_type=F32)
    start_row = jnp.dot(tot_row.astype(BF16), after, preferred_element_type=F32)
    marks[pl.ds(0, 8), :] = start_row.astype(I32)
    marks[pl.ds(8, 8), :] = tot_row.astype(I32)
    copy = pltpu.make_async_copy(marks, marks_s, sem)
    copy.start()
    ua = iota((nj, nj + owners), 0)
    ub = iota((nj, nj + owners), 1)
    upper = jnp.where((ua < ub) | (ub >= nj), 1.0, 0.0).astype(BF16)
    for t in range(nt):
        hot = hots[pl.ds(t * owners, owners), :]
        r = jnp.dot(hot, upper, preferred_element_type=F32)
        both = jnp.concatenate([base] * (nj // owners), axis=1)
        mine = jnp.where(owner_iota == owner_ref[pl.ds(t, 1), :], r[:, :nj] + both, 0.0)
        place[pl.ds(t, 1), :] = jnp.sum(mine, axis=0, keepdims=True)
        base = base + r[:, nj:]
    group = 4
    acc = None
    for c in range(nt // group):
        for u in range(group):
            t = c * group + u
            pos = place[pl.ds(t, 1), :].astype(I32)
            high = pos >> 8
            low = pos & 255
            top, rest = split2(jnp.concatenate([payload0[pl.ds(t * 8, 8), :], payload1[pl.ds(t * 8, 8), :]], axis=1))
            words = jnp.concatenate([top, rest], axis=0)
            high16 = jnp.broadcast_to(high, (16, nj))
            for h in range(32):
                left[pl.ds(h * 16, 16), pl.ds(u * nj, nj)] = jnp.where(high16 == h, words, 0.0).astype(BF16)
            right[:, pl.ds(u * nj, nj)] = jnp.where(iota((nj, nj), 0) == low, 1.0, 0.0).astype(BF16)
        part = lax.dot_general(left[...], right[...], ROWS_DIMS, preferred_element_type=F32)
        acc = part if acc is None else acc + part
    for h in range(32):
        both = acc[h * 16:h * 16 + 8] + acc[h * 16 + 8:h * 16 + 16]
        sorted_rows[2 * h] = both[:, :128]
        sorted_rows[2 * h + 1] = both[:, 128:]
    zero = jnp.zeros((8, 128), F32)
    sorted_rows[64] = zero
    sorted_rows[65] = zero
    copy.wait()
    lane = iota((8, 128), 1)

    def expand(o, carry):
        start = marks_s[0, o]
        count = marks_s[8, o]
        blk = start >> 7
        off = start & 127
        turn = (128 - off) & 127
        v0 = pltpu.roll(sorted_rows[blk], turn, 1)
        v1 = pltpu.roll(sorted_rows[blk + 1], turn, 1)
        v2 = pltpu.roll(sorted_rows[blk + 2], turn, 1)
        keep = lane < 128 - off
        out_ref[o, pl.ds(0, 8), :] = jnp.where(lane < count, jnp.where(keep, v0, v1), 0.0)
        out_ref[o, pl.ds(8, 8), :] = jnp.where(lane < count - 128, jnp.where(keep, v1, v2), 0.0)
        return carry

    lax.fori_loop(0, owners, expand, 0, unroll=8)


def pack(fluxes, weights, source, owner, cell):
    nf, nn, ne = fluxes.shape
    nt, _, nj = weights.shape
    owners = 128
    return pl.pallas_call(
        pack_kernel,
        out_shape=jax.ShapeDtypeStruct((owners, 16, 128), F32),
        grid=(1,),
        in_specs=[
            pl.BlockSpec((nf * nn, ne), lambda i: (0, 0)),
            pl.BlockSpec((nt * nn, 128), lambda i: (0, 0)),
            pl.BlockSpec((nt * nn, 128), lambda i: (0, 1)),
            pl.BlockSpec((1, nj), lambda i: (0, 0)),
            pl.BlockSpec((nt, nj), lambda i: (0, 0)),
            pl.BlockSpec((nt, nj), lambda i: (0, 0)),
        ],
        out_specs=pl.BlockSpec((owners, 16, 128), lambda i: (0, 0, 0)),
        scratch_shapes=[
            pltpu.VMEM((nf * nn, 128), F32),
            pltpu.VMEM((nf * nn, 128), F32),
            pltpu.VMEM((nt * 8, 128), F32),
            pltpu.VMEM((nt * 8, 128), F32),
            pltpu.VMEM((nt * owners, nj), BF16),
            pltpu.VMEM((nt, nj), F32),
            pltpu.VMEM((66, 8, 128), F32),
            pltpu.VMEM((512, 4 * nj), BF16),
            pltpu.VMEM((256, 4 * nj), BF16),
            pltpu.VMEM((16, 128), I32),
            pltpu.SMEM((16, 128), I32),
            pltpu.SemaphoreType.DMA,
        ],
        compiler_params=pltpu.CompilerParams(vmem_limit_bytes=48 * 2**20),
        name="pack",
    )(fluxes.reshape(nf * nn, ne), weights.reshape(nt * nn, nj), weights.reshape(nt * nn, nj), source.reshape(1, nj), owner, cell)


def deposit_kernel(rows_ref, out_ref, low_ref, high_ref, left, right):
    senders = rows_ref.shape[0]
    fields = 6
    group = 4
    x_iota = iota((64, 256), 0)
    y_iota = iota((256, 256), 0)
    out_ref[...] = jnp.zeros_like(out_ref)

    def step(c, carry):
        for u in range(group):
            d = c * group + u
            tile = jnp.concatenate([rows_ref[d, pl.ds(0, 8), :], rows_ref[d, pl.ds(8, 8), :]], axis=1)
            cell = tile[6:7].astype(I32)
            xh = x_iota == (cell >> 8)
            top, rest = split2(tile)
            for f in range(fields):
                left[pl.ds(f * 64, 64), pl.ds(u * 256, 256)] = jnp.where(xh, top[f:f + 1], 0.0).astype(BF16)
                left[pl.ds((fields + f) * 64, 64), pl.ds(u * 256, 256)] = jnp.where(xh, rest[f:f + 1], 0.0).astype(BF16)
            right[:, pl.ds(u * 256, 256)] = jnp.where(y_iota == (cell & 255), 1.0, 0.0).astype(BF16)
        part = lax.dot_general(left[...], right[...], ROWS_DIMS, preferred_element_type=F32)
        out_ref[...] += part[:fields * 64] + part[fields * 64:]
        return carry

    lax.fori_loop(0, senders // group, step, 0)
    for f in range(fields):
        low_ref[f] = out_ref[pl.ds(f * 64, HALO), :]
        high_ref[f] = out_ref[pl.ds(f * 64 + 60, HALO), :]


def deposit(rows):
    return pl.pallas_call(
        deposit_kernel,
        out_shape=(
            jax.ShapeDtypeStruct((6 * 64, 256), F32),
            jax.ShapeDtypeStruct((6, HALO, 256), F32),
            jax.ShapeDtypeStruct((6, HALO, 256), F32),
        ),
        scratch_shapes=[pltpu.VMEM((768, 1024), BF16), pltpu.VMEM((256, 1024), BF16)],
        compiler_params=pltpu.CompilerParams(vmem_limit_bytes=48 * 2**20),
        name="deposit",
    )(rows)


def join_rows(own, bottom, top):
    return jnp.concatenate([own, jnp.concatenate([bottom, top], axis=0)], axis=0)


def edges_kernel(state_ref, wet_ref, low_ref, high_ref):
    planes = state_ref.shape[0]
    rows = state_ref.shape[1]
    for ref, at in ((low_ref, 0), (high_ref, rows - HALO)):
        wet = wet_ref[pl.ds(at, HALO), :].astype(F32)
        for p in range(planes):
            ref[p] = state_ref[p, pl.ds(at, HALO), :] * wet
        ref[planes] = wet


def edges(state, wet):
    planes, rows, cols = state.shape
    shape = jax.ShapeDtypeStruct((planes + 1, HALO, cols), F32)
    return pl.pallas_call(edges_kernel, out_shape=(shape, shape), name="edges")(state, wet)


def strip_lanes(plane, group, lane):
    near = pltpu.roll(plane[:, :128], (group * 16 + 4) % 128, 1)
    far = pltpu.roll(plane[:, 128:], (group * 16 + 8 - 124) % 128, 1)
    at = lane - group * 16
    out = jnp.where((at >= 4) & (at < 8), near, 0.0)
    return jnp.where((at >= 8) & (at < 12), far, out)


def repeat_groups(x):
    for turn in (16, 32, 64):
        x = x + pltpu.roll(x, turn, 1)
    return x


def strips_kernel(state_ref, wet_ref, top_ref, bottom_ref, out_ref):
    planes = state_ref.shape[0]
    lane = iota((72, 128), 1)
    wet = wet_ref[...].astype(F32)
    for f in range(FIELDS):
        total = None
        for k in range(LEVELS):
            p = f * LEVELS + k
            plane = join_rows(state_ref[p] * wet, bottom_ref[p], top_ref[p])
            piece = strip_lanes(plane, k, lane)
            total = piece if total is None else total + piece
        out_ref[f] = total
    plane = join_rows(wet, bottom_ref[planes], top_ref[planes])
    out_ref[FIELDS] = repeat_groups(strip_lanes(plane, 0, lane))


def strips(state, wet, top, bottom):
    return pl.pallas_call(strips_kernel, out_shape=jax.ShapeDtypeStruct((FIELDS + 1, 72, 128), F32), name="strips")(state, wet, top, bottom)


def forcing_strips_kernel(forcing_ref, top_ref, bottom_ref, out_ref):
    lane = iota((72, 128), 1)
    total = None
    for f in range(6):
        plane = join_rows(forcing_ref[pl.ds(f * 64, 64), :], bottom_ref[f], top_ref[f])
        piece = strip_lanes(plane, f, lane)
        total = piece if total is None else total + piece
    out_ref[...] = total


def forcing_strips(forcing, top, bottom):
    return pl.pallas_call(forcing_strips_kernel, out_shape=jax.ShapeDtypeStruct((72, 128), F32), name="forcing_strips")(forcing, top, bottom)


def ocean_kernel(state_ref, wet_ref, top_ref, bottom_ref, own_ref, from_left_ref, from_right_ref,
                 forcing_ref, ftop_ref, fbottom_ref, fown_ref, fleft_ref, fright_ref, cor_ref, scor_ref,
                 out_ref, va, vb, wets, forc, ta, tb, swet, sforc):
    planes = FIELDS * LEVELS
    wet = wet_ref[...].astype(F32)
    wets[...] = join_rows(wet, bottom_ref[planes], top_ref[planes])
    for p in range(planes):
        va[p, pl.ds(8, 64), :] = state_ref[p] * wet
        ring = jnp.concatenate([bottom_ref[p], top_ref[p]], axis=0)
        va[p, pl.ds(72, 8), :] = ring
        va[p, pl.ds(0, 8), :] = ring
        va[p, pl.ds(80, 8), :] = va[p, pl.ds(8, 8), :]
    for f in range(6):
        plane = join_rows(forcing_ref[pl.ds(f * 64, 64), :], fbottom_ref[f], ftop_ref[f])
        if f == 5:
            mixing = plane * plane
            plane = mixing / (1.0 + mixing)
        forc[f] = plane
    lane = iota((72, 128), 1)
    slot = lane & 15

    def merge(own, left, right):
        out = jnp.where(slot < 4, pltpu.roll(left, 120, 1), own)
        return jnp.where(slot >= 12, pltpu.roll(right, 8, 1), out)

    for f in range(FIELDS + 1):
        whole = merge(own_ref[f], from_left_ref[f], from_right_ref[f])
        if f == FIELDS:
            swet[...] = whole
        else:
            ta[f, pl.ds(8, 72), :] = whole
            ta[f, pl.ds(0, 8), :] = whole[64:]
            ta[f, pl.ds(80, 8), :] = whole[:8]
    fwhole = merge(fown_ref[...], fleft_ref[...], fright_ref[...])
    for f in range(6):
        one = jnp.where(lane < 16, pltpu.roll(fwhole, (128 - 16 * f) % 128, 1), 0.0)
        one = repeat_groups(one)
        if f == 5:
            mixing = one * one
            one = mixing / (1.0 + mixing)
        sforc[f] = one

    lane8 = iota((8, 128), 1)
    first, last_lane = lane8 == 0, lane8 == 127
    cor = 0.1 * cor_ref[...]
    scor = 0.1 * scor_ref[...]
    level8 = (lane8 >> 4).astype(F32)
    fade = jnp.exp(-level8)
    solar = 0.05 * jnp.exp(-0.5 * level8)
    surface = jnp.where(lane8 < 16, 0.1, 0.0)
    decay = [math.exp(-k) for k in range(LEVELS)]
    heat = [0.05 * math.exp(-0.5 * k) for k in range(LEVELS)]

    row8 = iota((8, 128), 0)

    def halves(x):
        return x[:, :128], x[:, 128:]

    def row_shift(here, there, row, turn):
        return pltpu.roll(jnp.where(row8 == row, there, here), turn, 0)

    def main_step(src, strip, dst, final):
        def tile(i, carry):
            r = pl.multiple_of(i * 8, 8)
            wet2 = halves(wets[pl.ds(r, 8), :])
            force = [halves(forc[f, pl.ds(r, 8), :]) for f in range(6)]
            cor2 = halves(cor)
            edge = [strip[f, pl.ds(r + 8, 8), :] for f in range(FIELDS)]
            center = [halves(src[f * LEVELS, pl.ds(r + 8, 8), :]) for f in range(FIELDS)]
            below = [None] * FIELDS
            px = [0.0, 0.0]
            py = [0.0, 0.0]
            for k in range(LEVELS):
                dx, dy, sums = [], [], []
                for f in range(FIELDS):
                    p = f * LEVELS + k
                    lo, hi = center[f]
                    east = [row_shift(c, n, 0, 7) for c, n in zip(center[f], halves(src[p, pl.ds(r + 16, 8), :]))]
                    west = [row_shift(c, n, 7, 1) for c, n in zip(center[f], halves(src[p, pl.ds(r, 8), :]))]
                    lo_s, hi_s = pltpu.roll(lo, 1, 1), pltpu.roll(hi, 1, 1)
                    lo_n, hi_n = pltpu.roll(lo, 127, 1), pltpu.roll(hi, 127, 1)
                    edge_s = pltpu.roll(edge[f], (128 - (k * 16 + 3)) % 128, 1)
                    edge_n = pltpu.roll(edge[f], (127 - (k * 16 + 12)) % 128, 1)
                    south = (jnp.where(first, edge_s, lo_s), jnp.where(first, lo_s, hi_s))
                    north = (jnp.where(last_lane, hi_n, lo_n), jnp.where(last_lane, edge_n, hi_n))
                    dx.append([east[h] - west[h] for h in range(2)])
                    dy.append([north[h] - south[h] for h in range(2)])
                    sums.append([(east[h] + west[h]) + (north[h] + south[h]) for h in range(2)])
                for h in range(2):
                    px[h] = px[h] + (dx[3][h] - dx[2][h])
                    py[h] = py[h] + (dy[3][h] - dy[2][h])
                hu = [0.05 * center[0][h] for h in range(2)]
                hv = [0.05 * center[1][h] for h in range(2)]
                if k + 1 < LEVELS:
                    upper = [halves(src[f * LEVELS + k + 1, pl.ds(r + 8, 8), :]) for f in range(FIELDS)]
                    diffusivity = [0.03 + (0.12 * decay[k]) * force[5][h] for h in range(2)]
                for f in range(FIELDS):
                    result = []
                    for h in range(2):
                        value = 0.9 * center[f][h] + 0.025 * sums[f][h]
                        value = value - hu[h] * dx[f][h] - hv[h] * dy[f][h]
                        if below[f] is not None:
                            value = value - below[f][h]
                        if f == 0:
                            value = value + cor2[h] * center[1][h] - 0.01 * px[h]
                        if f == 1:
                            value = value - cor2[h] * center[0][h] - 0.01 * py[h]
                        if f == 2:
                            value = value + heat[k] * force[3][h]
                        if k == 0:
                            value = value + 0.1 * force[(0, 1, 2, 4)[f]][h]
                        result.append(value)
                    if k + 1 < LEVELS:
                        flow = [diffusivity[h] * (upper[f][h] - center[f][h]) for h in range(2)]
                        result = [result[h] + flow[h] for h in range(2)]
                        below[f] = flow
                    whole = jnp.concatenate([wet2[h] * result[h] for h in range(2)], axis=1)
                    if final:
                        dst[f * LEVELS + k, pl.ds(r, 8), :] = whole
                    else:
                        dst[f * LEVELS + k, pl.ds(r + 8, 8), :] = whole
                if k + 1 < LEVELS:
                    center = upper
            return carry

        lax.fori_loop(0, 8 if final else 9, tile, 0)
        if not final:
            for p in range(planes):
                dst[p, pl.ds(0, 8), :] = dst[p, pl.ds(72, 8), :]
                dst[p, pl.ds(80, 8), :] = dst[p, pl.ds(8, 8), :]

    def scan_levels(x):
        for turn in (16, 32, 64):
            x = x + jnp.where(lane8 >= turn, pltpu.roll(x, turn, 1), 0.0)
        return x

    def strip_step(src, dst):
        def tile(i, carry):
            r = pl.multiple_of(i * 8, 8)
            force = [sforc[f, pl.ds(r, 8), :] for f in range(6)]
            center = [src[f, pl.ds(r + 8, 8), :] for f in range(FIELDS)]
            east = [row_shift(c, src[f, pl.ds(r + 16, 8), :], 0, 7) for f, c in enumerate(center)]
            west = [row_shift(c, src[f, pl.ds(r, 8), :], 7, 1) for f, c in enumerate(center)]
            north = [pltpu.roll(c, 127, 1) for c in center]
            south = [pltpu.roll(c, 1, 1) for c in center]
            dx = [a - b for a, b in zip(east, west)]
            dy = [a - b for a, b in zip(north, south)]
            px = scan_levels(dx[3] - dx[2])
            py = scan_levels(dy[3] - dy[2])
            diffusivity = jnp.where(lane8 < 112, 0.03 + 0.12 * fade * force[5], 0.0)
            hu, hv = 0.05 * center[0], 0.05 * center[1]
            for f in range(FIELDS):
                value = 0.9 * center[f] + 0.025 * ((east[f] + west[f]) + (north[f] + south[f]))
                value = value - hu * dx[f] - hv * dy[f]
                flow = diffusivity * (pltpu.roll(center[f], 112, 1) - center[f])
                value = value + flow - pltpu.roll(flow, 16, 1)
                if f == 0:
                    value = value + scor * center[1] - 0.01 * px
                if f == 1:
                    value = value - scor * center[0] - 0.01 * py
                if f == 2:
                    value = value + solar * force[3]
                value = value + surface * force[(0, 1, 2, 4)[f]]
                dst[f, pl.ds(r + 8, 8), :] = swet[pl.ds(r, 8), :] * value
            return carry

        lax.fori_loop(0, 9, tile, 0)
        for f in range(FIELDS):
            dst[f, pl.ds(0, 8), :] = dst[f, pl.ds(72, 8), :]
            dst[f, pl.ds(80, 8), :] = dst[f, pl.ds(8, 8), :]

    source, other, strip, strip_other = va, vb, ta, tb
    for step in range(STEPS):
        final = step == STEPS - 1
        main_step(source, strip, out_ref if final else other, final)
        if not final:
            strip_step(strip, strip_other)
            source, other, strip, strip_other = other, source, strip_other, strip


def ocean(*args):
    state = args[0]
    planes = state.shape[0]
    return pl.pallas_call(
        ocean_kernel,
        out_shape=jax.ShapeDtypeStruct(state.shape, F32),
        scratch_shapes=[
            pltpu.VMEM((planes, 88, 256), F32),
            pltpu.VMEM((planes, 88, 256), F32),
            pltpu.VMEM((72, 256), F32),
            pltpu.VMEM((6, 72, 256), F32),
            pltpu.VMEM((FIELDS, 88, 128), F32),
            pltpu.VMEM((FIELDS, 88, 128), F32),
            pltpu.VMEM((72, 128), F32),
            pltpu.VMEM((6, 72, 128), F32),
        ],
        compiler_params=pltpu.CompilerParams(vmem_limit_bytes=48 * 2**20),
        name="ocean",
    )(*args)


def shift(x, axis, step):
    n = lax.axis_size(axis)
    pairs = [(i, i + step) for i in range(n) if 0 <= i + step < n]
    return lax.ppermute(x, axis, pairs)


def per_device(fluxes, remap_weights, source_elem, owner_map, target_cell, ocean_state, wet_mask):
    state = ocean_state.reshape(FIELDS * LEVELS, 64, 256)
    low, high = edges(state, wet_mask)
    top = shift(high, "gx", 1)
    bottom = shift(low, "gx", -1)
    own = strips(state, wet_mask, top, bottom)
    from_left = shift(own, "gy", 1)
    from_right = shift(own, "gy", -1)
    sent = pack(fluxes, remap_weights, source_elem, owner_map, target_cell)
    rows = lax.all_to_all(sent, ("gx", "gy"), split_axis=0, concat_axis=0, tiled=True)
    forcing, flow, fhigh = deposit(rows)
    ftop = shift(fhigh, "gx", 1)
    fbottom = shift(flow, "gx", -1)
    fown = forcing_strips(forcing, ftop, fbottom)
    fleft = shift(fown, "gy", 1)
    fright = shift(fown, "gy", -1)
    base = (lax.axis_index("gy") * 256).astype(F32)
    total = 256.0 * lax.axis_size("gy")

    def coriolis(y):
        return 0.5 + 0.5 * (y / total - 0.5)

    cor = coriolis(base + jnp.arange(256, dtype=F32))[None]
    slot = jnp.arange(128, dtype=I32) & 15
    scor = coriolis(base + jnp.where(slot < 8, slot - 4, slot + 244).astype(F32))[None]
    out = ocean(state, wet_mask, top, bottom, own, from_left, from_right,
                forcing, ftop, fbottom, fown, fleft, fright, cor, scor)
    return out.reshape(ocean_state.shape)


def solution(mesh):
    in_specs = (
        P(None, None, ("gx", "gy")),
        P(None, None, ("gx", "gy")),
        P(("gx", "gy")),
        P(None, ("gx", "gy")),
        P(None, ("gx", "gy")),
        P(None, None, "gx", "gy"),
        P("gx", "gy"),
    )
    out_specs = P(None, None, "gx", "gy")
    return jax.shard_map(per_device, mesh=mesh, in_specs=in_specs, out_specs=out_specs, check_vma=False)
```

```python
import math

import jax
import jax.numpy as jnp
from jax import lax
from jax.sharding import PartitionSpec as P
from jax.experimental import pallas as pl
from jax.experimental.pallas import tpu as pltpu
F32, BF16, I32 = jnp.float32, jnp.bfloat16, jnp.int32
FIELDS, LEVELS, HALO, STEPS = 4, 8, 4, 4
ROWS_DIMS = (((1,), (1,)), ((), ()))


def iota(shape, dim, dtype=I32):
    return lax.broadcasted_iota(dtype, shape, dim)


def split2(v):
    top = v.astype(BF16).astype(F32)
    return top, v - top


def side(axis, even, odd):
    return jnp.where(lax.axis_index(axis) % 2 == 0, even, odd)


def remap_kernel(flux_hbm, weight_hbm, source_hbm, cell_hbm, state_hbm, wet_hbm,
                 payload0, payload1, first_ref, second_ref,
                 flux_ref, weight0_ref, weight1_ref, source_ref, cell_ref, low_ref, high_ref,
                 wet_low, wet_high, gathered0, gathered1, sems):
    nt, nj = cell_ref.shape
    fields, nodes = 6, 16
    planes, rows, _ = state_hbm.shape
    copies = [
        pltpu.make_async_copy(source_hbm, source_ref, sems.at[0]),
        pltpu.make_async_copy(flux_hbm, flux_ref, sems.at[1]),
        pltpu.make_async_copy(weight_hbm.at[:, pl.ds(0, 128)], weight0_ref, sems.at[2]),
        pltpu.make_async_copy(weight_hbm.at[:, pl.ds(128, 128)], weight1_ref, sems.at[3]),
        pltpu.make_async_copy(cell_hbm, cell_ref, sems.at[4]),
        pltpu.make_async_copy(wet_hbm.at[pl.ds(0, 8)], wet_low, sems.at[5]),
        pltpu.make_async_copy(wet_hbm.at[pl.ds(rows - 8, 8)], wet_high, sems.at[6]),
        pltpu.make_async_copy(state_hbm.at[:, pl.ds(0, 8)], low_ref, sems.at[7]),
        pltpu.make_async_copy(state_hbm.at[:, pl.ds(rows - 8, 8)], high_ref, sems.at[8]),
    ]
    for copy in copies:
        copy.start()
    copies[0].wait()
    copies[1].wait()
    flux = flux_ref[...]
    f1 = flux.astype(BF16)
    r1 = flux - f1.astype(F32)
    f2 = r1.astype(BF16)
    f3 = (r1 - f2.astype(F32)).astype(BF16)
    elem_hot = jnp.where(iota((flux.shape[1], nj), 0) == source_ref[...], 1.0, 0.0).astype(BF16)
    g = jnp.dot(f1, elem_hot, preferred_element_type=F32)
    g = g + jnp.dot(f2, elem_hot, preferred_element_type=F32)
    g = g + jnp.dot(f3, elem_hot, preferred_element_type=F32)
    gathered0[...] = g[:, :128]
    gathered1[...] = g[:, 128:]
    for copy in copies[2:]:
        copy.wait()
    halves = ((weight0_ref, gathered0, payload0), (weight1_ref, gathered1, payload1))
    for half, (weight_ref, gathered, payload) in enumerate(halves):
        for f in range(fields):
            acc = None
            for s in range(nodes):
                term = weight_ref[pl.ds(s, nt, stride=nodes), :] * gathered[pl.ds(f * nodes + s, 1), :]
                acc = term if acc is None else acc + term
            payload[pl.ds(f, nt, stride=8), :] = acc
        payload[pl.ds(6, nt, stride=8), :] = cell_ref[:, pl.ds(half * 128, 128)].astype(F32)
        payload[pl.ds(7, nt, stride=8), :] = jnp.zeros((nt, 128), F32)
    wl = wet_low[...].astype(F32)[:HALO]
    wh = wet_high[...].astype(F32)[8 - HALO:]
    for p in range(planes):
        lo = low_ref[p][:HALO] * wl
        hi = high_ref[p][8 - HALO:] * wh
        first_ref[p] = side("gx", hi, lo)
        second_ref[p] = side("gx", lo, hi)
    first_ref[planes] = side("gx", wh, wl)
    second_ref[planes] = side("gx", wl, wh)


def remap(fluxes, weights, source, cell, state, wet):
    nf, nn, ne = fluxes.shape
    nt, _, nj = weights.shape
    planes, rows, cols = state.shape
    pay = jax.ShapeDtypeStruct((nt * 8, 128), F32)
    edge = jax.ShapeDtypeStruct((planes + 1, HALO, cols), F32)
    return pl.pallas_call(
        remap_kernel,
        out_shape=(pay, pay, edge, edge),
        in_specs=[pl.BlockSpec(memory_space=pltpu.HBM)] * 6,
        scratch_shapes=[
            pltpu.VMEM((nf * nn, ne), F32),
            pltpu.VMEM((nt * nn, 128), F32),
            pltpu.VMEM((nt * nn, 128), F32),
            pltpu.VMEM((1, nj), I32),
            pltpu.VMEM((nt, nj), I32),
            pltpu.VMEM((planes, 8, cols), F32),
            pltpu.VMEM((planes, 8, cols), F32),
            pltpu.VMEM((8, cols), I32),
            pltpu.VMEM((8, cols), I32),
            pltpu.VMEM((nf * nn, 128), F32),
            pltpu.VMEM((nf * nn, 128), F32),
            pltpu.SemaphoreType.DMA((9,)),
        ],
        compiler_params=pltpu.CompilerParams(vmem_limit_bytes=32 * 2**20),
        name="remap",
    )(fluxes.reshape(nf * nn, ne), weights.reshape(nt * nn, nj), source.reshape(1, nj), cell, state, wet)


def pack_kernel(payload0, payload1, owner_ref, out_ref, hots, place, sorted_rows, left, right, marks, marks_s, sem):
    nt, nj = owner_ref.shape
    owners = out_ref.shape[0]
    owner_iota = iota((owners, nj), 0)
    total = None
    for t in range(nt):
        hot = jnp.where(owner_iota == owner_ref[pl.ds(t, 1), :], 1.0, 0.0).astype(BF16)
        hots[pl.ds(t * owners, owners), :] = hot
        total = hot if total is None else total + hot
    ones = jnp.ones((nj, owners), BF16)
    tot_col = jnp.dot(total, ones, preferred_element_type=F32)
    tot_row = lax.dot_general(jnp.ones((8, nj), BF16), total, ROWS_DIMS, preferred_element_type=F32)
    a = iota((owners, owners), 0)
    b = iota((owners, owners), 1)
    before = jnp.where(b < a, 1.0, 0.0).astype(BF16)
    after = jnp.where(a < b, 1.0, 0.0).astype(BF16)
    base = jnp.dot(before, tot_col.astype(BF16), preferred_element_type=F32)
    start_row = jnp.dot(tot_row.astype(BF16), after, preferred_element_type=F32)
    marks[pl.ds(0, 8), :] = start_row.astype(I32)
    marks[pl.ds(8, 8), :] = tot_row.astype(I32)
    copy = pltpu.make_async_copy(marks, marks_s, sem)
    copy.start()
    ua = iota((nj, nj + owners), 0)
    ub = iota((nj, nj + owners), 1)
    upper = jnp.where((ua < ub) | (ub >= nj), 1.0, 0.0).astype(BF16)
    for t in range(nt):
        hot = hots[pl.ds(t * owners, owners), :]
        r = jnp.dot(hot, upper, preferred_element_type=F32)
        both = jnp.concatenate([base] * (nj // owners), axis=1)
        mine = jnp.where(owner_iota == owner_ref[pl.ds(t, 1), :], r[:, :nj] + both, 0.0)
        place[pl.ds(t, 1), :] = jnp.sum(mine, axis=0, keepdims=True)
        base = base + r[:, nj:]
    group = 4
    acc = None
    for c in range(nt // group):
        for u in range(group):
            t = c * group + u
            pos = place[pl.ds(t, 1), :].astype(I32)
            high = pos >> 8
            low = pos & 255
            top, rest = split2(jnp.concatenate([payload0[pl.ds(t * 8, 8), :], payload1[pl.ds(t * 8, 8), :]], axis=1))
            words = jnp.concatenate([top, rest], axis=0)
            high16 = jnp.broadcast_to(high, (16, nj))
            for h in range(32):
                left[pl.ds(h * 16, 16), pl.ds(u * nj, nj)] = jnp.where(high16 == h, words, 0.0).astype(BF16)
            right[:, pl.ds(u * nj, nj)] = jnp.where(iota((nj, nj), 0) == low, 1.0, 0.0).astype(BF16)
        part = lax.dot_general(left[...], right[...], ROWS_DIMS, preferred_element_type=F32)
        acc = part if acc is None else acc + part
    for h in range(32):
        both = acc[h * 16:h * 16 + 8] + acc[h * 16 + 8:h * 16 + 16]
        sorted_rows[2 * h] = both[:, :128]
        sorted_rows[2 * h + 1] = both[:, 128:]
    zero = jnp.zeros((8, 128), F32)
    sorted_rows[64] = zero
    sorted_rows[65] = zero
    copy.wait()
    lane = iota((8, 128), 1)

    def expand(o, carry):
        start = marks_s[0, o]
        count = marks_s[8, o]
        blk = start >> 7
        off = start & 127
        turn = (128 - off) & 127
        v0 = pltpu.roll(sorted_rows[blk], turn, 1)
        v1 = pltpu.roll(sorted_rows[blk + 1], turn, 1)
        v2 = pltpu.roll(sorted_rows[blk + 2], turn, 1)
        keep = lane < 128 - off
        out_ref[o, pl.ds(0, 8), :] = jnp.where(lane < count, jnp.where(keep, v0, v1), 0.0)
        out_ref[o, pl.ds(8, 8), :] = jnp.where(lane < count - 128, jnp.where(keep, v1, v2), 0.0)
        return carry

    lax.fori_loop(0, owners, expand, 0, unroll=8)


def pack(payload0, payload1, owner):
    nt, nj = owner.shape
    owners = 128
    return pl.pallas_call(
        pack_kernel,
        out_shape=jax.ShapeDtypeStruct((owners, 16, 128), F32),
        scratch_shapes=[
            pltpu.VMEM((nt * owners, nj), BF16),
            pltpu.VMEM((nt, nj), F32),
            pltpu.VMEM((66, 8, 128), F32),
            pltpu.VMEM((512, 4 * nj), BF16),
            pltpu.VMEM((256, 4 * nj), BF16),
            pltpu.VMEM((16, 128), I32),
            pltpu.SMEM((16, 128), I32),
            pltpu.SemaphoreType.DMA,
        ],
        compiler_params=pltpu.CompilerParams(vmem_limit_bytes=32 * 2**20),
        name="pack",
    )(payload0, payload1, owner)


def deposit_kernel(rows_ref, out_ref, first_ref, second_ref, left, right):
    senders = rows_ref.shape[0]
    fields = 6
    group = 4
    x_iota = iota((64, 256), 0)
    y_iota = iota((256, 256), 0)
    out_ref[...] = jnp.zeros_like(out_ref)

    def step(c, carry):
        for u in range(group):
            d = c * group + u
            tile = jnp.concatenate([rows_ref[d, pl.ds(0, 8), :], rows_ref[d, pl.ds(8, 8), :]], axis=1)
            cell = tile[6:7].astype(I32)
            xh = x_iota == (cell >> 8)
            top, rest = split2(tile)
            for f in range(fields):
                left[pl.ds(f * 64, 64), pl.ds(u * 256, 256)] = jnp.where(xh, top[f:f + 1], 0.0).astype(BF16)
                left[pl.ds((fields + f) * 64, 64), pl.ds(u * 256, 256)] = jnp.where(xh, rest[f:f + 1], 0.0).astype(BF16)
            right[:, pl.ds(u * 256, 256)] = jnp.where(y_iota == (cell & 255), 1.0, 0.0).astype(BF16)
        part = lax.dot_general(left[...], right[...], ROWS_DIMS, preferred_element_type=F32)
        out_ref[...] += part[:fields * 64] + part[fields * 64:]
        return carry

    lax.fori_loop(0, senders // group, step, 0)
    for f in range(fields):
        low = out_ref[pl.ds(f * 64, 8), :][:HALO]
        high = out_ref[pl.ds(f * 64 + 56, 8), :][8 - HALO:]
        first_ref[f] = side("gx", high, low)
        second_ref[f] = side("gx", low, high)


def deposit(rows):
    return pl.pallas_call(
        deposit_kernel,
        out_shape=(
            jax.ShapeDtypeStruct((6 * 64, 256), F32),
            jax.ShapeDtypeStruct((6, HALO, 256), F32),
            jax.ShapeDtypeStruct((6, HALO, 256), F32),
        ),
        scratch_shapes=[pltpu.VMEM((768, 1024), BF16), pltpu.VMEM((256, 1024), BF16)],
        compiler_params=pltpu.CompilerParams(vmem_limit_bytes=32 * 2**20),
        name="deposit",
    )(rows)


def join_rows(own, bottom, top):
    return jnp.concatenate([own, jnp.concatenate([bottom, top], axis=0)], axis=0)


def ends(first, second, inside):
    me, count = lax.axis_index("gx"), lax.axis_size("gx")
    bottom, top = side("gx", first, second), side("gx", second, first)
    if inside:
        bottom = jnp.where(me == count - 1, 0.0, bottom)
        top = jnp.where(me == 0, 0.0, top)
    return bottom, top


def strip_lanes(plane, group, lane):
    near = pltpu.roll(plane[:, :128], (group * 16 + 4) % 128, 1)
    far = pltpu.roll(plane[:, 128:], (group * 16 + 8 - 124) % 128, 1)
    at = lane - group * 16
    out = jnp.where((at >= 4) & (at < 8), near, 0.0)
    return jnp.where((at >= 8) & (at < 12), far, out)


def repeat_groups(x):
    for turn in (16, 32, 64):
        x = x + pltpu.roll(x, turn, 1)
    return x


def strips_kernel(state_hbm, wet_ref, first_ref, second_ref, out_ref, all_ref, wets_ref, sem):
    planes = state_hbm.shape[0]
    copy = pltpu.make_async_copy(state_hbm, all_ref.at[:, pl.ds(8, 64)], sem)
    copy.start()
    lane = iota((72, 128), 1)
    wet = wet_ref[...].astype(F32)
    plane = join_rows(wet, *ends(first_ref[planes], second_ref[planes], True))
    wets_ref[...] = plane
    out_ref[FIELDS] = repeat_groups(strip_lanes(plane, 0, lane))
    copy.wait()
    for f in range(FIELDS):
        total = None
        for k in range(LEVELS):
            p = f * LEVELS + k
            own = all_ref[p, pl.ds(8, 64), :] * wet
            ring = jnp.concatenate(ends(first_ref[p], second_ref[p], True), axis=0)
            all_ref[p, pl.ds(8, 64), :] = own
            all_ref[p, pl.ds(72, 8), :] = ring
            all_ref[p, pl.ds(0, 8), :] = ring
            all_ref[p, pl.ds(80, 8), :] = own[:8]
            piece = strip_lanes(jnp.concatenate([own, ring], axis=0), k, lane)
            total = piece if total is None else total + piece
        out_ref[f] = total


def strips(state, wet, first, second):
    planes, rows, cols = state.shape
    return pl.pallas_call(
        strips_kernel,
        out_shape=(
            jax.ShapeDtypeStruct((FIELDS + 1, 72, 128), F32),
            jax.ShapeDtypeStruct((planes, 88, cols), F32),
            jax.ShapeDtypeStruct((72, cols), F32),
        ),
        in_specs=[pl.BlockSpec(memory_space=pltpu.HBM)] + [pl.BlockSpec(memory_space=pltpu.VMEM)] * 3,
        scratch_shapes=[pltpu.SemaphoreType.DMA],
        compiler_params=pltpu.CompilerParams(vmem_limit_bytes=32 * 2**20),
        name="strips",
    )(state, wet, first, second)


def forcing_strips_kernel(forcing_ref, first_ref, second_ref, out_ref):
    lane = iota((72, 128), 1)
    total = None
    for f in range(6):
        plane = join_rows(forcing_ref[pl.ds(f * 64, 64), :], *ends(first_ref[f], second_ref[f], False))
        piece = strip_lanes(plane, f, lane)
        total = piece if total is None else total + piece
    out_ref[...] = total


def forcing_strips(forcing, first, second):
    return pl.pallas_call(
        forcing_strips_kernel,
        out_shape=jax.ShapeDtypeStruct((72, 128), F32),
        compiler_params=pltpu.CompilerParams(vmem_limit_bytes=32 * 2**20),
        name="forcing_strips",
    )(forcing, first, second)


def ocean_kernel(va, wets, own_ref, sfirst_ref, ssecond_ref, forcing_ref, ffirst_ref, fsecond_ref,
                 fown_ref, fsfirst_ref, fssecond_ref, out_ref, vb, vc, forc, ta, tb, swet, sforc):
    planes = FIELDS * LEVELS
    for f in range(6):
        plane = join_rows(forcing_ref[pl.ds(f * 64, 64), :], *ends(ffirst_ref[f], fsecond_ref[f], False))
        if f == 5:
            mixing = plane * plane
            plane = mixing / (1.0 + mixing)
        forc[f] = plane
    gy, gy_size = lax.axis_index("gy"), lax.axis_size("gy")
    lane = iota((72, 128), 1)
    slot = lane & 15

    def merge(own, first, second):
        left = jnp.where(gy == 0, 0.0, side("gy", second, first))
        right = jnp.where(gy == gy_size - 1, 0.0, side("gy", first, second))
        out = jnp.where(slot < 4, pltpu.roll(left, 120, 1), own)
        return jnp.where(slot >= 12, pltpu.roll(right, 8, 1), out)

    for f in range(FIELDS + 1):
        whole = merge(own_ref[f], sfirst_ref[f], ssecond_ref[f])
        if f == FIELDS:
            swet[...] = whole
        else:
            ta[f, pl.ds(8, 72), :] = whole
            ta[f, pl.ds(0, 8), :] = whole[64:]
            ta[f, pl.ds(80, 8), :] = whole[:8]
    fwhole = merge(fown_ref[...], fsfirst_ref[...], fssecond_ref[...])
    for f in range(6):
        one = jnp.where(lane < 16, pltpu.roll(fwhole, (128 - 16 * f) % 128, 1), 0.0)
        one = repeat_groups(one)
        if f == 5:
            mixing = one * one
            one = mixing / (1.0 + mixing)
        sforc[f] = one

    lane8 = iota((8, 128), 1)
    first, last_lane = lane8 == 0, lane8 == 127
    base_y = (gy * 256).astype(F32)
    total_y = 256.0 * gy_size

    def coriolis(y):
        return 0.1 * (0.5 + 0.5 * ((base_y + y.astype(F32)) / total_y - 0.5))

    cor = coriolis(iota((8, 256), 1))
    slot8 = lane8 & 15
    scor = coriolis(jnp.where(slot8 < 8, slot8 - 4, slot8 + 244))
    level8 = (lane8 >> 4).astype(F32)
    fade = jnp.exp(-level8)
    solar = 0.05 * jnp.exp(-0.5 * level8)
    surface = jnp.where(lane8 < 16, 0.1, 0.0)
    decay = [math.exp(-k) for k in range(LEVELS)]
    heat = [0.05 * math.exp(-0.5 * k) for k in range(LEVELS)]

    row8 = iota((8, 128), 0)

    def halves(x):
        return x[:, :128], x[:, 128:]

    def row_shift(here, there, row, turn):
        return pltpu.roll(jnp.where(row8 == row, there, here), turn, 0)

    def main_step(src, strip, dst, final):
        def tile(i, carry):
            r = pl.multiple_of(i * 8, 8)
            wet2 = halves(wets[pl.ds(r, 8), :])
            force = [halves(forc[f, pl.ds(r, 8), :]) for f in range(6)]
            cor2 = halves(cor)
            edge = [strip[f, pl.ds(r + 8, 8), :] for f in range(FIELDS)]
            center = [halves(src[f * LEVELS, pl.ds(r + 8, 8), :]) for f in range(FIELDS)]
            below = [None] * FIELDS
            px = [0.0, 0.0]
            py = [0.0, 0.0]
            for k in range(LEVELS):
                dx, dy, sums = [], [], []
                for f in range(FIELDS):
                    p = f * LEVELS + k
                    lo, hi = center[f]
                    east = [row_shift(c, n, 0, 7) for c, n in zip(center[f], halves(src[p, pl.ds(r + 16, 8), :]))]
                    west = [row_shift(c, n, 7, 1) for c, n in zip(center[f], halves(src[p, pl.ds(r, 8), :]))]
                    lo_s, hi_s = pltpu.roll(lo, 1, 1), pltpu.roll(hi, 1, 1)
                    lo_n, hi_n = pltpu.roll(lo, 127, 1), pltpu.roll(hi, 127, 1)
                    edge_s = pltpu.roll(edge[f], (128 - (k * 16 + 3)) % 128, 1)
                    edge_n = pltpu.roll(edge[f], (127 - (k * 16 + 12)) % 128, 1)
                    south = (jnp.where(first, edge_s, lo_s), jnp.where(first, lo_s, hi_s))
                    north = (jnp.where(last_lane, hi_n, lo_n), jnp.where(last_lane, edge_n, hi_n))
                    dx.append([east[h] - west[h] for h in range(2)])
                    dy.append([north[h] - south[h] for h in range(2)])
                    sums.append([(east[h] + west[h]) + (north[h] + south[h]) for h in range(2)])
                for h in range(2):
                    px[h] = px[h] + (dx[3][h] - dx[2][h])
                    py[h] = py[h] + (dy[3][h] - dy[2][h])
                hu = [0.05 * center[0][h] for h in range(2)]
                hv = [0.05 * center[1][h] for h in range(2)]
                if k + 1 < LEVELS:
                    upper = [halves(src[f * LEVELS + k + 1, pl.ds(r + 8, 8), :]) for f in range(FIELDS)]
                    diffusivity = [0.03 + (0.12 * decay[k]) * force[5][h] for h in range(2)]
                for f in range(FIELDS):
                    result = []
                    for h in range(2):
                        value = 0.9 * center[f][h] + 0.025 * sums[f][h]
                        value = value - hu[h] * dx[f][h] - hv[h] * dy[f][h]
                        if below[f] is not None:
                            value = value - below[f][h]
                        if f == 0:
                            value = value + cor2[h] * center[1][h] - 0.01 * px[h]
                        if f == 1:
                            value = value - cor2[h] * center[0][h] - 0.01 * py[h]
                        if f == 2:
                            value = value + heat[k] * force[3][h]
                        if k == 0:
                            value = value + 0.1 * force[(0, 1, 2, 4)[f]][h]
                        result.append(value)
                    if k + 1 < LEVELS:
                        flow = [diffusivity[h] * (upper[f][h] - center[f][h]) for h in range(2)]
                        result = [result[h] + flow[h] for h in range(2)]
                        below[f] = flow
                    whole = jnp.concatenate([wet2[h] * result[h] for h in range(2)], axis=1)
                    if final:
                        dst[f * LEVELS + k, pl.ds(r, 8), :] = whole
                    else:
                        dst[f * LEVELS + k, pl.ds(r + 8, 8), :] = whole
                if k + 1 < LEVELS:
                    center = upper
            return carry

        lax.fori_loop(0, 8 if final else 9, tile, 0)
        if not final:
            for p in range(planes):
                dst[p, pl.ds(0, 8), :] = dst[p, pl.ds(72, 8), :]
                dst[p, pl.ds(80, 8), :] = dst[p, pl.ds(8, 8), :]

    def scan_levels(x):
        for turn in (16, 32, 64):
            x = x + jnp.where(lane8 >= turn, pltpu.roll(x, turn, 1), 0.0)
        return x

    def strip_step(src, dst):
        def tile(i, carry):
            r = pl.multiple_of(i * 8, 8)
            force = [sforc[f, pl.ds(r, 8), :] for f in range(6)]
            center = [src[f, pl.ds(r + 8, 8), :] for f in range(FIELDS)]
            east = [row_shift(c, src[f, pl.ds(r + 16, 8), :], 0, 7) for f, c in enumerate(center)]
            west = [row_shift(c, src[f, pl.ds(r, 8), :], 7, 1) for f, c in enumerate(center)]
            north = [pltpu.roll(c, 127, 1) for c in center]
            south = [pltpu.roll(c, 1, 1) for c in center]
            dx = [a - b for a, b in zip(east, west)]
            dy = [a - b for a, b in zip(north, south)]
            px = scan_levels(dx[3] - dx[2])
            py = scan_levels(dy[3] - dy[2])
            diffusivity = jnp.where(lane8 < 112, 0.03 + 0.12 * fade * force[5], 0.0)
            hu, hv = 0.05 * center[0], 0.05 * center[1]
            for f in range(FIELDS):
                value = 0.9 * center[f] + 0.025 * ((east[f] + west[f]) + (north[f] + south[f]))
                value = value - hu * dx[f] - hv * dy[f]
                flow = diffusivity * (pltpu.roll(center[f], 112, 1) - center[f])
                value = value + flow - pltpu.roll(flow, 16, 1)
                if f == 0:
                    value = value + scor * center[1] - 0.01 * px
                if f == 1:
                    value = value - scor * center[0] - 0.01 * py
                if f == 2:
                    value = value + solar * force[3]
                value = value + surface * force[(0, 1, 2, 4)[f]]
                dst[f, pl.ds(r + 8, 8), :] = swet[pl.ds(r, 8), :] * value
            return carry

        lax.fori_loop(0, 9, tile, 0)
        for f in range(FIELDS):
            dst[f, pl.ds(0, 8), :] = dst[f, pl.ds(72, 8), :]
            dst[f, pl.ds(80, 8), :] = dst[f, pl.ds(8, 8), :]

    source, strip, strip_other = va, ta, tb
    for step in range(STEPS):
        final = step == STEPS - 1
        target = out_ref if final else (vb, vc)[step % 2]
        main_step(source, strip, target, final)
        if not final:
            strip_step(strip, strip_other)
            source, strip, strip_other = target, strip_other, strip


def ocean(*args):
    planes = FIELDS * LEVELS
    return pl.pallas_call(
        ocean_kernel,
        out_shape=jax.ShapeDtypeStruct((planes, 64, 256), F32),
        scratch_shapes=[
            pltpu.VMEM((planes, 88, 256), F32),
            pltpu.VMEM((planes, 88, 256), F32),
            pltpu.VMEM((6, 72, 256), F32),
            pltpu.VMEM((FIELDS, 88, 128), F32),
            pltpu.VMEM((FIELDS, 88, 128), F32),
            pltpu.VMEM((72, 128), F32),
            pltpu.VMEM((6, 72, 128), F32),
        ],
        compiler_params=pltpu.CompilerParams(vmem_limit_bytes=32 * 2**20),
        name="ocean",
    )(*args)


def swap(first, second, axis):
    n = lax.axis_size(axis)
    pairs = [(i, i ^ 1) for i in range(n)]
    others = [(i, (i + (1 if i % 2 else n - 1)) % n) for i in range(n)]
    return lax.ppermute(first, axis, pairs), lax.ppermute(second, axis, others)


def per_device(fluxes, remap_weights, source_elem, owner_map, target_cell, ocean_state, wet_mask):
    state = ocean_state.reshape(FIELDS * LEVELS, 64, 256)
    payload0, payload1, first, second = remap(fluxes, remap_weights, source_elem, target_cell, state, wet_mask)
    first, second = swap(first, second, "gx")
    sent = pack(payload0, payload1, owner_map)
    rows = lax.all_to_all(sent, ("gx", "gy"), split_axis=0, concat_axis=0, tiled=True)
    own, everything, wets = strips(state, wet_mask, first, second)
    sfirst, ssecond = swap(own, own, "gy")
    forcing, ffirst, fsecond = deposit(rows)
    ffirst, fsecond = swap(ffirst, fsecond, "gx")
    fown = forcing_strips(forcing, ffirst, fsecond)
    fsfirst, fssecond = swap(fown, fown, "gy")
    out = ocean(everything, wets, own, sfirst, ssecond, forcing, ffirst, fsecond, fown, fsfirst, fssecond)
    return out.reshape(ocean_state.shape)


def solution(mesh):
    in_specs = (
        P(None, None, ("gx", "gy")),
        P(None, None, ("gx", "gy")),
        P(("gx", "gy")),
        P(None, ("gx", "gy")),
        P(None, ("gx", "gy")),
        P(None, None, "gx", "gy"),
        P("gx", "gy"),
    )
    out_specs = P(None, None, "gx", "gy")
    return jax.shard_map(per_device, mesh=mesh, in_specs=in_specs, out_specs=out_specs, check_vma=False)
```

```python
import math

import jax
import jax.numpy as jnp
from jax import lax
from jax.sharding import PartitionSpec as P
from jax.experimental import pallas as pl
from jax.experimental.pallas import tpu as pltpu
F32, BF16, I32 = jnp.float32, jnp.bfloat16, jnp.int32
FIELDS, LEVELS, HALO, STEPS = 4, 8, 4, 4
GROUP = 32
TIGHT = 66 * 10**6
PACK_GROUP = 16
ROWS_DIMS = (((1,), (1,)), ((), ()))


def iota(shape, dim, dtype=I32):
    return lax.broadcasted_iota(dtype, shape, dim)


def split2(v):
    top = v.astype(BF16).astype(F32)
    return top, v - top


def spread16(row):
    return jnp.broadcast_to(row, (16, row.shape[1])).astype(BF16)


def lines16(count, width):
    steps = iota((16, width), 0).astype(F32)
    return [(steps + 16.0 * i).astype(BF16) for i in range(count)]


def side(axis, even, odd):
    return jnp.where(lax.axis_index(axis) % 2 == 0, even, odd)


def remap_kernel(flux_hbm, weight_hbm, source_hbm, cell_hbm, state_hbm, wet_hbm,
                 payload0, payload1, first_ref, second_ref,
                 flux_ref, weight0_ref, weight1_ref, source_ref, cell_ref, low_ref, high_ref,
                 wet_low, wet_high, gathered0, gathered1, sems):
    nt, nj = cell_ref.shape
    fields, nodes = 6, 16
    planes, rows, _ = state_hbm.shape
    copies = [
        pltpu.make_async_copy(source_hbm, source_ref, sems.at[0]),
        pltpu.make_async_copy(flux_hbm, flux_ref, sems.at[1]),
        pltpu.make_async_copy(weight_hbm.at[:, pl.ds(0, 128)], weight0_ref, sems.at[2]),
        pltpu.make_async_copy(weight_hbm.at[:, pl.ds(128, 128)], weight1_ref, sems.at[3]),
        pltpu.make_async_copy(cell_hbm, cell_ref, sems.at[4]),
        pltpu.make_async_copy(wet_hbm.at[pl.ds(0, 8)], wet_low, sems.at[5]),
        pltpu.make_async_copy(wet_hbm.at[pl.ds(rows - 8, 8)], wet_high, sems.at[6]),
        pltpu.make_async_copy(state_hbm.at[:, pl.ds(0, 8)], low_ref, sems.at[7]),
        pltpu.make_async_copy(state_hbm.at[:, pl.ds(rows - 8, 8)], high_ref, sems.at[8]),
    ]
    for copy in copies:
        copy.start()
    copies[0].wait()
    copies[1].wait()
    flux = flux_ref[...]
    f1 = flux.astype(BF16)
    r1 = flux - f1.astype(F32)
    f2 = r1.astype(BF16)
    f3 = (r1 - f2.astype(F32)).astype(BF16)
    elem_hot = jnp.where(iota((flux.shape[1], nj), 0) == source_ref[...], 1.0, 0.0).astype(BF16)
    g = jnp.dot(f1, elem_hot, preferred_element_type=F32)
    g = g + jnp.dot(f2, elem_hot, preferred_element_type=F32)
    g = g + jnp.dot(f3, elem_hot, preferred_element_type=F32)
    gathered0[...] = g[:, :128]
    gathered1[...] = g[:, 128:]
    for copy in copies[2:]:
        copy.wait()
    halves = ((weight0_ref, gathered0, payload0), (weight1_ref, gathered1, payload1))
    for half, (weight_ref, gathered, payload) in enumerate(halves):
        for f in range(fields):
            acc = None
            for s in range(nodes):
                term = weight_ref[pl.ds(s, nt, stride=nodes), :] * gathered[pl.ds(f * nodes + s, 1), :]
                acc = term if acc is None else acc + term
            payload[pl.ds(f, nt, stride=8), :] = acc
        payload[pl.ds(6, nt, stride=8), :] = cell_ref[:, pl.ds(half * 128, 128)].astype(F32)
        payload[pl.ds(7, nt, stride=8), :] = jnp.zeros((nt, 128), F32)
    wl = wet_low[...].astype(F32)[:HALO]
    wh = wet_high[...].astype(F32)[8 - HALO:]
    for p in range(planes):
        lo = low_ref[p][:HALO] * wl
        hi = high_ref[p][8 - HALO:] * wh
        first_ref[p] = side("gx", hi, lo)
        second_ref[p] = side("gx", lo, hi)
    first_ref[planes] = side("gx", wh, wl)
    second_ref[planes] = side("gx", wl, wh)


def remap(fluxes, weights, source, cell, state, wet):
    nf, nn, ne = fluxes.shape
    nt, _, nj = weights.shape
    planes, rows, cols = state.shape
    pay = jax.ShapeDtypeStruct((nt * 8, 128), F32)
    edge = jax.ShapeDtypeStruct((planes + 1, HALO, cols), F32)
    return pl.pallas_call(
        remap_kernel,
        out_shape=(pay, pay, edge, edge),
        in_specs=[pl.BlockSpec(memory_space=pltpu.HBM)] * 6,
        scratch_shapes=[
            pltpu.VMEM((nf * nn, ne), F32),
            pltpu.VMEM((nt * nn, 128), F32),
            pltpu.VMEM((nt * nn, 128), F32),
            pltpu.VMEM((1, nj), I32),
            pltpu.VMEM((nt, nj), I32),
            pltpu.VMEM((planes, 8, cols), F32),
            pltpu.VMEM((planes, 8, cols), F32),
            pltpu.VMEM((8, cols), I32),
            pltpu.VMEM((8, cols), I32),
            pltpu.VMEM((nf * nn, 128), F32),
            pltpu.VMEM((nf * nn, 128), F32),
            pltpu.SemaphoreType.DMA((9,)),
        ],
        compiler_params=pltpu.CompilerParams(vmem_limit_bytes=TIGHT),
        name="remap",
    )(fluxes.reshape(nf * nn, ne), weights.reshape(nt * nn, nj), source.reshape(1, nj), cell, state, wet)


def pack_kernel(payload0, payload1, owner_ref, out_hbm, out_ref, out_sems, hots, place, sorted_rows, left, right, marks, marks_s, sem):
    nt, nj = owner_ref.shape
    owners = out_ref.shape[0]
    owner_iota = iota((owners, nj), 0)
    one, zero = jnp.ones((16, nj), BF16), jnp.zeros((16, nj), BF16)
    lines = lines16(nj // 16, nj)
    totals = [zero] * (owners // 16)
    for t in range(nt):
        o16 = spread16(owner_ref[pl.ds(t, 1), :].astype(F32))
        for i in range(owners // 16):
            hot = jnp.where(o16 == lines[i], one, zero)
            hots[pl.ds(t * owners + i * 16, 16), :] = hot
            totals[i] = totals[i] + hot
    total = jnp.concatenate(totals, axis=0)
    ones = jnp.ones((nj, owners), BF16)
    tot_col = jnp.dot(total, ones, preferred_element_type=F32)
    tot_row = lax.dot_general(jnp.ones((8, nj), BF16), total, ROWS_DIMS, preferred_element_type=F32)
    a = iota((owners, owners), 0)
    b = iota((owners, owners), 1)
    before = jnp.where(b < a, 1.0, 0.0).astype(BF16)
    after = jnp.where(a < b, 1.0, 0.0).astype(BF16)
    base = jnp.dot(before, tot_col.astype(BF16), preferred_element_type=F32)
    start_row = jnp.dot(tot_row.astype(BF16), after, preferred_element_type=F32)
    marks[pl.ds(0, 8), :] = start_row.astype(I32)
    marks[pl.ds(8, 8), :] = tot_row.astype(I32)
    copy = pltpu.make_async_copy(marks, marks_s, sem)
    copy.start()
    ua = iota((nj, nj + owners), 0)
    ub = iota((nj, nj + owners), 1)
    upper = jnp.where((ua < ub) | (ub >= nj), 1.0, 0.0).astype(BF16)
    for t in range(nt):
        hot = hots[pl.ds(t * owners, owners), :]
        r = jnp.dot(hot, upper, preferred_element_type=F32)
        both = jnp.concatenate([base] * (nj // owners), axis=1)
        mine = jnp.where(owner_iota == owner_ref[pl.ds(t, 1), :], r[:, :nj] + both, 0.0)
        place[pl.ds(t, 1), :] = jnp.sum(mine, axis=0, keepdims=True)
        base = base + r[:, nj:]
    acc = None
    for c in range(nt // PACK_GROUP):
        for u in range(PACK_GROUP):
            t = c * PACK_GROUP + u
            at = pl.ds(u * nj, nj)
            pos = place[pl.ds(t, 1), :].astype(I32)
            high16 = spread16((pos >> 8).astype(F32))
            low16 = spread16((pos & 255).astype(F32))
            top, rest = split2(jnp.concatenate([payload0[pl.ds(t * 8, 8), :], payload1[pl.ds(t * 8, 8), :]], axis=1))
            words = jnp.concatenate([top, rest], axis=0).astype(BF16)
            for h in range(32):
                left[pl.ds(h * 16, 16), at] = jnp.where(high16 == float(h), words, zero)
            for i in range(nj // 16):
                right[pl.ds(i * 16, 16), at] = jnp.where(low16 == lines[i], one, zero)
        part = lax.dot_general(left[...], right[...], ROWS_DIMS, preferred_element_type=F32)
        acc = part if acc is None else acc + part
    for h in range(32):
        both = acc[h * 16:h * 16 + 8] + acc[h * 16 + 8:h * 16 + 16]
        sorted_rows[2 * h] = both[:, :128]
        sorted_rows[2 * h + 1] = both[:, 128:]
    zero = jnp.zeros((8, 128), F32)
    sorted_rows[64] = zero
    sorted_rows[65] = zero
    sorted_rows[66] = zero
    copy.wait()
    lane = iota((8, 128), 1)

    def expand(o, carry):
        start = marks_s[0, o]
        count = marks_s[8, o]
        blk = start >> 7
        off = start & 127
        turn = (128 - off) & 127
        v0 = pltpu.roll(sorted_rows[blk], turn, 1)
        v1 = pltpu.roll(sorted_rows[blk + 1], turn, 1)
        v2 = pltpu.roll(sorted_rows[blk + 2], turn, 1)
        keep = lane < 128 - off
        out_ref[o, pl.ds(0, 8), :] = jnp.where(lane < count, jnp.where(keep, v0, v1), 0.0)
        out_ref[o, pl.ds(8, 8), :] = jnp.where(lane < count - 128, jnp.where(keep, v1, v2), 0.0)
        return carry

    pieces = [pl.ds(i * 16, 16) for i in range(owners // 16)]
    sends = [pltpu.make_async_copy(out_ref.at[at], out_hbm.at[at], out_sems.at[i]) for i, at in enumerate(pieces)]
    for i, send in enumerate(sends):
        lax.fori_loop(i * 16, i * 16 + 16, expand, 0, unroll=8)
        send.start()
    for send in sends:
        send.wait()


def pack(payload0, payload1, owner):
    nt, nj = owner.shape
    owners = 128
    return pl.pallas_call(
        pack_kernel,
        out_shape=jax.ShapeDtypeStruct((owners, 16, 128), F32),
        out_specs=pl.BlockSpec(memory_space=pltpu.HBM),
        scratch_shapes=[
            pltpu.VMEM((owners, 16, 128), F32),
            pltpu.SemaphoreType.DMA((owners // 16,)),
            pltpu.VMEM((nt * owners, nj), BF16),
            pltpu.VMEM((nt, nj), F32),
            pltpu.VMEM((67, 8, 128), F32),
            pltpu.VMEM((512, PACK_GROUP * nj), BF16),
            pltpu.VMEM((256, PACK_GROUP * nj), BF16),
            pltpu.VMEM((16, 128), I32),
            pltpu.SMEM((16, 128), I32),
            pltpu.SemaphoreType.DMA,
        ],
        compiler_params=pltpu.CompilerParams(vmem_limit_bytes=TIGHT),
        name="pack",
    )(payload0, payload1, owner)


def deposit_kernel(rows_ref, out_ref, first_ref, second_ref, left, right):
    senders = rows_ref.shape[0]
    fields = 6
    group = GROUP
    one, zero = jnp.ones((16, 256), BF16), jnp.zeros((16, 256), BF16)
    lines = lines16(16, 256)
    out_ref[...] = jnp.zeros_like(out_ref)

    def step(c, carry):
        for u in range(group):
            d = c * group + u
            tile = jnp.concatenate([rows_ref[d, pl.ds(0, 8), :], rows_ref[d, pl.ds(8, 8), :]], axis=1)
            cell = tile[6:7].astype(I32)
            x16 = spread16((cell >> 8).astype(F32))
            y16 = spread16((cell & 255).astype(F32))
            top, rest = split2(tile)
            at = pl.ds(u * 256, 256)
            hots = [jnp.where(x16 == lines[i], one, zero) for i in range(4)]
            for part, values in enumerate((top, rest)):
                for f in range(fields):
                    v16 = spread16(values[f:f + 1])
                    for i in range(4):
                        left[pl.ds((part * fields + f) * 64 + i * 16, 16), at] = hots[i] * v16
            for i in range(16):
                right[pl.ds(i * 16, 16), at] = jnp.where(y16 == lines[i], one, zero)
        part = lax.dot_general(left[...], right[...], ROWS_DIMS, preferred_element_type=F32)
        out_ref[...] += part[:fields * 64] + part[fields * 64:]
        return carry

    lax.fori_loop(0, senders // group, step, 0)
    for f in range(fields):
        low = out_ref[pl.ds(f * 64, 8), :][:HALO]
        high = out_ref[pl.ds(f * 64 + 56, 8), :][8 - HALO:]
        first_ref[f] = side("gx", high, low)
        second_ref[f] = side("gx", low, high)


def deposit(rows):
    return pl.pallas_call(
        deposit_kernel,
        out_shape=(
            jax.ShapeDtypeStruct((6 * 64, 256), F32),
            jax.ShapeDtypeStruct((6, HALO, 256), F32),
            jax.ShapeDtypeStruct((6, HALO, 256), F32),
        ),
        scratch_shapes=[pltpu.VMEM((768, 256 * GROUP), BF16), pltpu.VMEM((256, 256 * GROUP), BF16)],
        compiler_params=pltpu.CompilerParams(vmem_limit_bytes=26 * 2**20),
        name="deposit",
    )(rows)


def join_rows(own, bottom, top):
    return jnp.concatenate([own, jnp.concatenate([bottom, top], axis=0)], axis=0)


def ends(first, second, inside):
    me, count = lax.axis_index("gx"), lax.axis_size("gx")
    bottom, top = side("gx", first, second), side("gx", second, first)
    if inside:
        bottom = jnp.where(me == count - 1, 0.0, bottom)
        top = jnp.where(me == 0, 0.0, top)
    return bottom, top


def strip_lanes(plane, group, lane):
    near = pltpu.roll(plane[:, :128], (group * 16 + 4) % 128, 1)
    far = pltpu.roll(plane[:, 128:], (group * 16 + 8 - 124) % 128, 1)
    at = lane - group * 16
    out = jnp.where((at >= 4) & (at < 8), near, 0.0)
    return jnp.where((at >= 8) & (at < 12), far, out)


def repeat_groups(x):
    for turn in (16, 32, 64):
        x = x + pltpu.roll(x, turn, 1)
    return x


def strips_kernel(state_ref, wet_ref, first_ref, second_ref, out_ref, wets_ref):
    planes = state_ref.shape[0]
    lane = iota((72, 128), 1)
    wet = wet_ref[...].astype(F32)
    plane = join_rows(wet, *ends(first_ref[planes], second_ref[planes], True))
    wets_ref[...] = plane
    out_ref[FIELDS] = repeat_groups(strip_lanes(plane, 0, lane))
    for f in range(FIELDS):
        total = None
        for k in range(LEVELS):
            p = f * LEVELS + k
            plane = join_rows(state_ref[p] * wet, *ends(first_ref[p], second_ref[p], True))
            piece = strip_lanes(plane, k, lane)
            total = piece if total is None else total + piece
        out_ref[f] = total


def strips(state, wet, first, second):
    planes, rows, cols = state.shape
    return pl.pallas_call(
        strips_kernel,
        out_shape=(
            jax.ShapeDtypeStruct((FIELDS + 1, 72, 128), F32),
            jax.ShapeDtypeStruct((72, cols), F32),
        ),
        compiler_params=pltpu.CompilerParams(vmem_limit_bytes=16 * 2**20),
        name="strips",
    )(state, wet, first, second)


def forcing_strips_kernel(forcing_ref, first_ref, second_ref, out_ref):
    lane = iota((72, 128), 1)
    total = None
    for f in range(6):
        plane = join_rows(forcing_ref[pl.ds(f * 64, 64), :], *ends(first_ref[f], second_ref[f], False))
        piece = strip_lanes(plane, f, lane)
        total = piece if total is None else total + piece
    out_ref[...] = total


def forcing_strips(forcing, first, second):
    return pl.pallas_call(
        forcing_strips_kernel,
        out_shape=jax.ShapeDtypeStruct((72, 128), F32),
        compiler_params=pltpu.CompilerParams(vmem_limit_bytes=8 * 2**20),
        name="forcing_strips",
    )(forcing, first, second)


def ocean_kernel(state_ref, first_ref, second_ref, wets, own_ref, sfirst_ref, ssecond_ref, forcing_ref, ffirst_ref, fsecond_ref,
                 fown_ref, fsfirst_ref, fssecond_ref, out_hbm, out_ref, out_sems, va, vb, vc, forc, ta, tb, swet, sforc):
    planes = FIELDS * LEVELS
    for p in range(planes):
        own = state_ref[p] * wets[pl.ds(0, 64), :]
        ring = jnp.concatenate(ends(first_ref[p], second_ref[p], True), axis=0)
        va[p, pl.ds(8, 64), :] = own
        va[p, pl.ds(72, 8), :] = ring
        va[p, pl.ds(0, 8), :] = ring
        va[p, pl.ds(80, 8), :] = own[:8]
    for f in range(6):
        plane = join_rows(forcing_ref[pl.ds(f * 64, 64), :], *ends(ffirst_ref[f], fsecond_ref[f], False))
        if f == 5:
            mixing = plane * plane
            plane = mixing / (1.0 + mixing)
        forc[f] = plane
    gy, gy_size = lax.axis_index("gy"), lax.axis_size("gy")
    lane = iota((72, 128), 1)
    slot = lane & 15

    def merge(own, first, second):
        left = jnp.where(gy == 0, 0.0, side("gy", second, first))
        right = jnp.where(gy == gy_size - 1, 0.0, side("gy", first, second))
        out = jnp.where(slot < 4, pltpu.roll(left, 120, 1), own)
        return jnp.where(slot >= 12, pltpu.roll(right, 8, 1), out)

    for f in range(FIELDS + 1):
        whole = merge(own_ref[f], sfirst_ref[f], ssecond_ref[f])
        if f == FIELDS:
            swet[...] = whole
        else:
            ta[f, pl.ds(8, 72), :] = whole
            ta[f, pl.ds(0, 8), :] = whole[64:]
            ta[f, pl.ds(80, 8), :] = whole[:8]
    fwhole = merge(fown_ref[...], fsfirst_ref[...], fssecond_ref[...])
    for f in range(6):
        one = jnp.where(lane < 16, pltpu.roll(fwhole, (128 - 16 * f) % 128, 1), 0.0)
        one = repeat_groups(one)
        if f == 5:
            mixing = one * one
            one = mixing / (1.0 + mixing)
        sforc[f] = one

    lane8 = iota((8, 128), 1)
    first, last_lane = lane8 == 0, lane8 == 127
    base_y = (gy * 256).astype(F32)
    total_y = 256.0 * gy_size

    def coriolis(y):
        return 0.1 * (0.5 + 0.5 * ((base_y + y.astype(F32)) / total_y - 0.5))

    cor = coriolis(iota((8, 256), 1))
    slot8 = lane8 & 15
    scor = coriolis(jnp.where(slot8 < 8, slot8 - 4, slot8 + 244))
    level8 = (lane8 >> 4).astype(F32)
    fade = jnp.exp(-level8)
    solar = 0.05 * jnp.exp(-0.5 * level8)
    surface = jnp.where(lane8 < 16, 0.1, 0.0)
    decay = [math.exp(-k) for k in range(LEVELS)]
    heat = [0.05 * math.exp(-0.5 * k) for k in range(LEVELS)]

    row8 = iota((8, 128), 0)

    def halves(x):
        return x[:, :128], x[:, 128:]

    def row_shift(here, there, row, turn):
        return pltpu.roll(jnp.where(row8 == row, there, here), turn, 0)

    def main_step(src, strip, dst, final):
        def tile(i, carry):
            r = pl.multiple_of(i * 8, 8)
            for half in range(2):
                here, there = pl.ds(half * 128, 128), pl.ds(128 - half * 128, 128)
                wet = wets[pl.ds(r, 8), here]
                force = [forc[f, pl.ds(r, 8), here] for f in range(6)]
                turn = cor[:, half * 128:half * 128 + 128]
                edge = [strip[f, pl.ds(r + 8, 8), :] for f in range(FIELDS)]
                center = [src[f * LEVELS, pl.ds(r + 8, 8), here] for f in range(FIELDS)]
                below = [None] * FIELDS
                px, py = 0.0, 0.0
                for k in range(LEVELS):
                    dx, dy, sums = [], [], []
                    for f in range(FIELDS):
                        p = f * LEVELS + k
                        c = center[f]
                        other = src[p, pl.ds(r + 8, 8), there]
                        east = row_shift(c, src[p, pl.ds(r + 16, 8), here], 0, 7)
                        west = row_shift(c, src[p, pl.ds(r, 8), here], 7, 1)
                        if half == 0:
                            outer = pltpu.roll(edge[f], (128 - (k * 16 + 3)) % 128, 1)
                            south = jnp.where(first, outer, pltpu.roll(c, 1, 1))
                            north = pltpu.roll(jnp.where(first, other, c), 127, 1)
                        else:
                            outer = pltpu.roll(edge[f], (127 - (k * 16 + 12)) % 128, 1)
                            south = pltpu.roll(jnp.where(last_lane, other, c), 1, 1)
                            north = jnp.where(last_lane, outer, pltpu.roll(c, 127, 1))
                        dx.append(east - west)
                        dy.append(north - south)
                        sums.append((east + west) + (north + south))
                    px = px + (dx[3] - dx[2])
                    py = py + (dy[3] - dy[2])
                    hu, hv = 0.05 * center[0], 0.05 * center[1]
                    if k + 1 < LEVELS:
                        upper = [src[f * LEVELS + k + 1, pl.ds(r + 8, 8), here] for f in range(FIELDS)]
                        diffusivity = 0.03 + (0.12 * decay[k]) * force[5]
                    for f in range(FIELDS):
                        value = 0.9 * center[f] + 0.025 * sums[f]
                        value = value - hu * dx[f] - hv * dy[f]
                        if below[f] is not None:
                            value = value - below[f]
                        if f == 0:
                            value = value + turn * center[1] - 0.01 * px
                        if f == 1:
                            value = value - turn * center[0] - 0.01 * py
                        if f == 2:
                            value = value + heat[k] * force[3]
                        if k == 0:
                            value = value + 0.1 * force[(0, 1, 2, 4)[f]]
                        if k + 1 < LEVELS:
                            below[f] = diffusivity * (upper[f] - center[f])
                            value = value + below[f]
                        dst[f * LEVELS + k, pl.ds(r if final else r + 8, 8), here] = wet * value
                    if k + 1 < LEVELS:
                        center = upper
            if final:
                done = pl.ds(r, 8)
                pltpu.make_async_copy(dst.at[:, done], out_hbm.at[:, done], out_sems.at[i]).start()
            return carry

        lax.fori_loop(0, 8 if final else 9, tile, 0)
        if final:
            for i in range(8):
                done = pl.ds(i * 8, 8)
                pltpu.make_async_copy(dst.at[:, done], out_hbm.at[:, done], out_sems.at[i]).wait()
        if not final:
            for p in range(planes):
                dst[p, pl.ds(0, 8), :] = dst[p, pl.ds(72, 8), :]
                dst[p, pl.ds(80, 8), :] = dst[p, pl.ds(8, 8), :]

    def scan_levels(x):
        for turn in (16, 32, 64):
            x = x + jnp.where(lane8 >= turn, pltpu.roll(x, turn, 1), 0.0)
        return x

    def strip_step(src, dst):
        def tile(i, carry):
            r = i * 8
            force = [sforc[f, pl.ds(r, 8), :] for f in range(6)]
            center = [src[f, pl.ds(r + 8, 8), :] for f in range(FIELDS)]
            east = [row_shift(c, src[f, pl.ds(r + 16, 8), :], 0, 7) for f, c in enumerate(center)]
            west = [row_shift(c, src[f, pl.ds(r, 8), :], 7, 1) for f, c in enumerate(center)]
            north = [pltpu.roll(c, 127, 1) for c in center]
            south = [pltpu.roll(c, 1, 1) for c in center]
            dx = [a - b for a, b in zip(east, west)]
            dy = [a - b for a, b in zip(north, south)]
            px = scan_levels(dx[3] - dx[2])
            py = scan_levels(dy[3] - dy[2])
            diffusivity = jnp.where(lane8 < 112, 0.03 + 0.12 * fade * force[5], 0.0)
            hu, hv = 0.05 * center[0], 0.05 * center[1]
            for f in range(FIELDS):
                value = 0.9 * center[f] + 0.025 * ((east[f] + west[f]) + (north[f] + south[f]))
                value = value - hu * dx[f] - hv * dy[f]
                flow = diffusivity * (pltpu.roll(center[f], 112, 1) - center[f])
                value = value + flow - pltpu.roll(flow, 16, 1)
                if f == 0:
                    value = value + scor * center[1] - 0.01 * px
                if f == 1:
                    value = value - scor * center[0] - 0.01 * py
                if f == 2:
                    value = value + solar * force[3]
                value = value + surface * force[(0, 1, 2, 4)[f]]
                dst[f, pl.ds(r + 8, 8), :] = swet[pl.ds(r, 8), :] * value
            return carry

        for i in range(9):
            tile(i, 0)
        for f in range(FIELDS):
            dst[f, pl.ds(0, 8), :] = dst[f, pl.ds(72, 8), :]
            dst[f, pl.ds(80, 8), :] = dst[f, pl.ds(8, 8), :]

    source, strip, strip_other = va, ta, tb
    for step in range(STEPS):
        final = step == STEPS - 1
        target = out_ref if final else (vb, vc)[step % 2]
        main_step(source, strip, target, final)
        if not final:
            strip_step(strip, strip_other)
            source, strip, strip_other = target, strip_other, strip


def ocean(*args):
    planes = FIELDS * LEVELS
    return pl.pallas_call(
        ocean_kernel,
        out_shape=jax.ShapeDtypeStruct((planes, 64, 256), F32),
        out_specs=pl.BlockSpec(memory_space=pltpu.HBM),
        scratch_shapes=[
            pltpu.VMEM((planes, 64, 256), F32),
            pltpu.SemaphoreType.DMA((8,)),
            pltpu.VMEM((planes, 88, 256), F32),
            pltpu.VMEM((planes, 88, 256), F32),
            pltpu.VMEM((planes, 88, 256), F32),
            pltpu.VMEM((6, 72, 256), F32),
            pltpu.VMEM((FIELDS, 88, 128), F32),
            pltpu.VMEM((FIELDS, 88, 128), F32),
            pltpu.VMEM((72, 128), F32),
            pltpu.VMEM((6, 72, 128), F32),
        ],
        compiler_params=pltpu.CompilerParams(vmem_limit_bytes=24 * 2**20),
        name="ocean",
    )(*args)


def swap(first, second, axis):
    n = lax.axis_size(axis)
    pairs = [(i, i ^ 1) for i in range(n)]
    others = [(i, (i + (1 if i % 2 else n - 1)) % n) for i in range(n)]
    return lax.ppermute(first, axis, pairs), lax.ppermute(second, axis, others)


def per_device(fluxes, remap_weights, source_elem, owner_map, target_cell, ocean_state, wet_mask):
    state = ocean_state.reshape(FIELDS * LEVELS, 64, 256)
    payload0, payload1, first, second = remap(fluxes, remap_weights, source_elem, target_cell, state, wet_mask)
    first, second = swap(first, second, "gx")
    sent = pack(payload0, payload1, owner_map)
    sent, first, second = lax.optimization_barrier((sent, first, second))
    rows = lax.all_to_all(sent, ("gx", "gy"), split_axis=0, concat_axis=0, tiled=True)
    own, wets = strips(state, wet_mask, first, second)
    sfirst, ssecond = swap(own, own, "gy")
    forcing, ffirst, fsecond = deposit(rows)
    ffirst, fsecond = swap(ffirst, fsecond, "gx")
    fown = forcing_strips(forcing, ffirst, fsecond)
    fsfirst, fssecond = swap(fown, fown, "gy")
    out = ocean(state, first, second, wets, own, sfirst, ssecond, forcing, ffirst, fsecond, fown, fsfirst, fssecond)
    return out.reshape(ocean_state.shape)


def solution(mesh):
    in_specs = (
        P(None, None, ("gx", "gy")),
        P(None, None, ("gx", "gy")),
        P(("gx", "gy")),
        P(None, ("gx", "gy")),
        P(None, ("gx", "gy")),
        P(None, None, "gx", "gy"),
        P("gx", "gy"),
    )
    out_specs = P(None, None, "gx", "gy")
    return jax.shard_map(per_device, mesh=mesh, in_specs=in_specs, out_specs=out_specs, check_vma=False)
```

```python
import math

import jax
import jax.numpy as jnp
from jax import lax
from jax.sharding import PartitionSpec as P
from jax.experimental import pallas as pl
from jax.experimental.pallas import tpu as pltpu
F32, BF16, I32 = jnp.float32, jnp.bfloat16, jnp.int32
FIELDS, LEVELS, HALO, STEPS = 4, 8, 4, 4
GROUP = 64
REST = 4096.0
F8 = jnp.float8_e4m3fn
TIGHT = 66 * 10**6
PACK_GROUP = 16
ROWS_DIMS = (((1,), (1,)), ((), ()))


def iota(shape, dim, dtype=I32):
    return lax.broadcasted_iota(dtype, shape, dim)


def split2(v):
    top = v.astype(BF16).astype(F32)
    return top, v - top


def spread16(row):
    return jnp.broadcast_to(row, (16, row.shape[1])).astype(BF16)


def lines16(count, width):
    steps = iota((16, width), 0).astype(F32)
    return [(steps + 16.0 * i).astype(BF16) for i in range(count)]


def side(axis, even, odd):
    return jnp.where(lax.axis_index(axis) % 2 == 0, even, odd)


def remap_kernel(flux_hbm, weight_hbm, source_hbm, cell_hbm, state_hbm, wet_hbm,
                 payload0, payload1, first_ref, second_ref,
                 flux_ref, weight0_ref, weight1_ref, source_ref, cell_ref, low_ref, high_ref,
                 wet_low, wet_high, gathered0, gathered1, sems):
    nt, nj = cell_ref.shape
    fields, nodes = 6, 16
    planes, rows, _ = state_hbm.shape
    copies = [
        pltpu.make_async_copy(source_hbm, source_ref, sems.at[0]),
        pltpu.make_async_copy(flux_hbm, flux_ref, sems.at[1]),
        pltpu.make_async_copy(weight_hbm.at[:, pl.ds(0, 128)], weight0_ref, sems.at[2]),
        pltpu.make_async_copy(weight_hbm.at[:, pl.ds(128, 128)], weight1_ref, sems.at[3]),
        pltpu.make_async_copy(cell_hbm, cell_ref, sems.at[4]),
        pltpu.make_async_copy(wet_hbm.at[pl.ds(0, 8)], wet_low, sems.at[5]),
        pltpu.make_async_copy(wet_hbm.at[pl.ds(rows - 8, 8)], wet_high, sems.at[6]),
        pltpu.make_async_copy(state_hbm.at[:, pl.ds(0, 8)], low_ref, sems.at[7]),
        pltpu.make_async_copy(state_hbm.at[:, pl.ds(rows - 8, 8)], high_ref, sems.at[8]),
    ]
    for copy in copies:
        copy.start()
    copies[0].wait()
    copies[1].wait()
    flux = flux_ref[...]
    f1 = flux.astype(BF16)
    r1 = flux - f1.astype(F32)
    f2 = r1.astype(BF16)
    f3 = (r1 - f2.astype(F32)).astype(BF16)
    elem_hot = jnp.where(iota((flux.shape[1], nj), 0) == source_ref[...], 1.0, 0.0).astype(BF16)
    g = jnp.dot(f1, elem_hot, preferred_element_type=F32)
    g = g + jnp.dot(f2, elem_hot, preferred_element_type=F32)
    g = g + jnp.dot(f3, elem_hot, preferred_element_type=F32)
    gathered0[...] = g[:, :128]
    gathered1[...] = g[:, 128:]
    for copy in copies[2:]:
        copy.wait()
    halves = ((weight0_ref, gathered0, payload0), (weight1_ref, gathered1, payload1))
    for half, (weight_ref, gathered, payload) in enumerate(halves):
        for f in range(fields):
            acc = None
            for s in range(nodes):
                term = weight_ref[pl.ds(s, nt, stride=nodes), :] * gathered[pl.ds(f * nodes + s, 1), :]
                acc = term if acc is None else acc + term
            payload[pl.ds(f, nt, stride=8), :] = acc
        cells = cell_ref[:, pl.ds(half * 128, 128)]
        payload[pl.ds(6, nt, stride=8), :] = (cells >> 8).astype(F32)
        payload[pl.ds(7, nt, stride=8), :] = (cells & 255).astype(F32)
    wl = wet_low[...].astype(F32)[:HALO]
    wh = wet_high[...].astype(F32)[8 - HALO:]
    for p in range(planes):
        lo = low_ref[p][:HALO] * wl
        hi = high_ref[p][8 - HALO:] * wh
        first_ref[p] = side("gx", hi, lo)
        second_ref[p] = side("gx", lo, hi)
    first_ref[planes] = side("gx", wh, wl)
    second_ref[planes] = side("gx", wl, wh)


def remap(fluxes, weights, source, cell, state, wet):
    nf, nn, ne = fluxes.shape
    nt, _, nj = weights.shape
    planes, rows, cols = state.shape
    pay = jax.ShapeDtypeStruct((nt * 8, 128), F32)
    edge = jax.ShapeDtypeStruct((planes + 1, HALO, cols), F32)
    return pl.pallas_call(
        remap_kernel,
        out_shape=(pay, pay, edge, edge),
        in_specs=[pl.BlockSpec(memory_space=pltpu.HBM)] * 6,
        scratch_shapes=[
            pltpu.VMEM((nf * nn, ne), F32),
            pltpu.VMEM((nt * nn, 128), F32),
            pltpu.VMEM((nt * nn, 128), F32),
            pltpu.VMEM((1, nj), I32),
            pltpu.VMEM((nt, nj), I32),
            pltpu.VMEM((planes, 8, cols), F32),
            pltpu.VMEM((planes, 8, cols), F32),
            pltpu.VMEM((8, cols), I32),
            pltpu.VMEM((8, cols), I32),
            pltpu.VMEM((nf * nn, 128), F32),
            pltpu.VMEM((nf * nn, 128), F32),
            pltpu.SemaphoreType.DMA((9,)),
        ],
        compiler_params=pltpu.CompilerParams(vmem_limit_bytes=TIGHT),
        name="remap",
    )(fluxes.reshape(nf * nn, ne), weights.reshape(nt * nn, nj), source.reshape(1, nj), cell, state, wet)


def pack_kernel(payload0, payload1, owner_ref, out_hbm, out_ref, out_sems, hots, place, sorted_rows, left, right, left8, right8, marks, marks_s, sem):
    nt, nj = owner_ref.shape
    owners = out_ref.shape[0]
    owner_iota = iota((owners, nj), 0)
    one, zero = jnp.ones((16, nj), BF16), jnp.zeros((16, nj), BF16)
    lines = lines16(nj // 16, nj)
    totals = [zero] * (owners // 16)
    for t in range(nt):
        o16 = spread16(owner_ref[pl.ds(t, 1), :].astype(F32))
        for i in range(owners // 16):
            hot = jnp.where(o16 == lines[i], one, zero)
            hots[pl.ds(t * owners + i * 16, 16), :] = hot
            totals[i] = totals[i] + hot
    total = jnp.concatenate(totals, axis=0)
    ones = jnp.ones((nj, owners), BF16)
    tot_col = jnp.dot(total, ones, preferred_element_type=F32)
    tot_row = lax.dot_general(jnp.ones((8, nj), BF16), total, ROWS_DIMS, preferred_element_type=F32)
    a = iota((owners, owners), 0)
    b = iota((owners, owners), 1)
    before = jnp.where(b < a, 1.0, 0.0).astype(BF16)
    after = jnp.where(a < b, 1.0, 0.0).astype(BF16)
    base = jnp.dot(before, tot_col.astype(BF16), preferred_element_type=F32)
    start_row = jnp.dot(tot_row.astype(BF16), after, preferred_element_type=F32)
    marks[pl.ds(0, 8), :] = start_row.astype(I32)
    marks[pl.ds(8, 8), :] = tot_row.astype(I32)
    copy = pltpu.make_async_copy(marks, marks_s, sem)
    copy.start()
    ua = iota((nj, nj + owners), 0)
    ub = iota((nj, nj + owners), 1)
    upper = jnp.where((ua < ub) | (ub >= nj), 1.0, 0.0).astype(BF16)
    for t in range(nt):
        hot = hots[pl.ds(t * owners, owners), :]
        r = jnp.dot(hot, upper, preferred_element_type=F32)
        both = jnp.concatenate([base] * (nj // owners), axis=1)
        mine = jnp.where(owner_iota == owner_ref[pl.ds(t, 1), :], r[:, :nj] + both, 0.0)
        place[pl.ds(t, 1), :] = jnp.sum(mine, axis=0, keepdims=True)
        base = base + r[:, nj:]
    pairs = [(2 * i + (iota((16, nj), 0) >> 3)).astype(F32).astype(BF16) for i in range(16)]
    acc = None
    for c in range(nt // PACK_GROUP):
        for u in range(PACK_GROUP):
            t = c * PACK_GROUP + u
            at = pl.ds(u * nj, nj)
            pos = place[pl.ds(t, 1), :].astype(I32)
            high16 = spread16((pos >> 8).astype(F32))
            low16 = spread16((pos & 255).astype(F32))
            top, rest = split2(jnp.concatenate([payload0[pl.ds(t * 8, 8), :], payload1[pl.ds(t * 8, 8), :]], axis=1))
            words = jnp.concatenate([top, top], axis=0).astype(BF16)
            small = (REST * jnp.concatenate([rest, rest], axis=0)).astype(BF16)
            for h in range(8):
                hots_here = [high16 == pairs[2 * h + i] for i in range(2)]
                for i in range(2):
                    left[pl.ds((2 * h + i) * 16, 16), at] = jnp.where(hots_here[i], words, zero)
                left8[pl.ds(h * 32, 32), at] = jnp.concatenate(
                    [jnp.where(hots_here[i], small, zero) for i in range(2)], axis=0
                ).astype(F8)
            for h in range(nj // 32):
                hots_here = [jnp.where(low16 == lines[2 * h + i], one, zero) for i in range(2)]
                for i in range(2):
                    right[pl.ds((2 * h + i) * 16, 16), at] = hots_here[i]
                right8[pl.ds(h * 32, 32), at] = jnp.concatenate(hots_here, axis=0).astype(F8)
        part = lax.dot_general(left[...], right[...], ROWS_DIMS, preferred_element_type=F32)
        small = lax.dot_general(left8[...], right8[...], ROWS_DIMS, preferred_element_type=F32)
        part = part + (1.0 / REST) * small
        acc = part if acc is None else acc + part
    for h in range(32):
        sorted_rows[2 * h] = acc[h * 8:h * 8 + 8, :128]
        sorted_rows[2 * h + 1] = acc[h * 8:h * 8 + 8, 128:]
    zero = jnp.zeros((8, 128), F32)
    sorted_rows[64] = zero
    sorted_rows[65] = zero
    sorted_rows[66] = zero
    copy.wait()
    lane = iota((8, 128), 1)

    def expand(o, carry):
        start = marks_s[0, o]
        count = marks_s[8, o]
        blk = start >> 7
        off = start & 127
        turn = (128 - off) & 127
        v0 = pltpu.roll(sorted_rows[blk], turn, 1)
        v1 = pltpu.roll(sorted_rows[blk + 1], turn, 1)
        v2 = pltpu.roll(sorted_rows[blk + 2], turn, 1)
        keep = lane < 128 - off
        out_ref[o, pl.ds(0, 8), :] = jnp.where(lane < count, jnp.where(keep, v0, v1), 0.0)
        out_ref[o, pl.ds(8, 8), :] = jnp.where(lane < count - 128, jnp.where(keep, v1, v2), 0.0)
        return carry

    pieces = [pl.ds(i * 16, 16) for i in range(owners // 16)]
    sends = [pltpu.make_async_copy(out_ref.at[at], out_hbm.at[at], out_sems.at[i]) for i, at in enumerate(pieces)]
    for i, send in enumerate(sends):
        lax.fori_loop(i * 16, i * 16 + 16, expand, 0, unroll=8)
        send.start()
    for send in sends:
        send.wait()


def pack(payload0, payload1, owner):
    nt, nj = owner.shape
    owners = 128
    return pl.pallas_call(
        pack_kernel,
        out_shape=jax.ShapeDtypeStruct((owners, 16, 128), F32),
        out_specs=pl.BlockSpec(memory_space=pltpu.HBM),
        scratch_shapes=[
            pltpu.VMEM((owners, 16, 128), F32),
            pltpu.SemaphoreType.DMA((owners // 16,)),
            pltpu.VMEM((nt * owners, nj), BF16),
            pltpu.VMEM((nt, nj), F32),
            pltpu.VMEM((67, 8, 128), F32),
            pltpu.VMEM((256, PACK_GROUP * nj), BF16),
            pltpu.VMEM((256, PACK_GROUP * nj), BF16),
            pltpu.VMEM((256, PACK_GROUP * nj), F8),
            pltpu.VMEM((256, PACK_GROUP * nj), F8),
            pltpu.VMEM((16, 128), I32),
            pltpu.SMEM((16, 128), I32),
            pltpu.SemaphoreType.DMA,
        ],
        compiler_params=pltpu.CompilerParams(vmem_limit_bytes=TIGHT),
        name="pack",
    )(payload0, payload1, owner)


def deposit_kernel(rows_ref, out_ref, first_ref, second_ref, left, right, left8, right8):
    senders = rows_ref.shape[0]
    fields = 6
    group = GROUP
    one, zero = jnp.ones((16, 256), BF16), jnp.zeros((16, 256), BF16)
    lines = lines16(16, 256)
    out_ref[...] = jnp.zeros_like(out_ref)

    def step(c, carry):
        for u in range(group):
            d = c * group + u
            tile = jnp.concatenate([rows_ref[d, pl.ds(0, 8), :], rows_ref[d, pl.ds(8, 8), :]], axis=1)
            x16 = spread16(tile[6:7])
            y16 = spread16(tile[7:8])
            top, rest = split2(tile)
            rest = REST * rest
            at = pl.ds(u * 256, 256)
            hots = [jnp.where(x16 == lines[i], one, zero) for i in range(4)]
            for f in range(fields):
                v16 = spread16(top[f:f + 1])
                r16 = spread16(rest[f:f + 1])
                for i in range(4):
                    left[pl.ds(f * 64 + i * 16, 16), at] = hots[i] * v16
                for i in range(2):
                    pair = jnp.concatenate([hots[2 * i] * r16, hots[2 * i + 1] * r16], axis=0)
                    left8[pl.ds(f * 64 + i * 32, 32), at] = pair.astype(F8)
            for i in range(8):
                pair = [jnp.where(y16 == lines[2 * i + j], one, zero) for j in range(2)]
                for j in range(2):
                    right[pl.ds((2 * i + j) * 16, 16), at] = pair[j]
                right8[pl.ds(i * 32, 32), at] = jnp.concatenate(pair, axis=0).astype(F8)
        part = lax.dot_general(left[...], right[...], ROWS_DIMS, preferred_element_type=F32)
        small = lax.dot_general(left8[...], right8[...], ROWS_DIMS, preferred_element_type=F32)
        out_ref[...] += part + (1.0 / REST) * small
        return carry

    lax.fori_loop(0, senders // group, step, 0)
    for f in range(fields):
        low = out_ref[pl.ds(f * 64, 8), :][:HALO]
        high = out_ref[pl.ds(f * 64 + 56, 8), :][8 - HALO:]
        first_ref[f] = side("gx", high, low)
        second_ref[f] = side("gx", low, high)


def deposit(rows):
    return pl.pallas_call(
        deposit_kernel,
        out_shape=(
            jax.ShapeDtypeStruct((6 * 64, 256), F32),
            jax.ShapeDtypeStruct((6, HALO, 256), F32),
            jax.ShapeDtypeStruct((6, HALO, 256), F32),
        ),
        scratch_shapes=[
            pltpu.VMEM((384, 256 * GROUP), BF16),
            pltpu.VMEM((256, 256 * GROUP), BF16),
            pltpu.VMEM((384, 256 * GROUP), F8),
            pltpu.VMEM((256, 256 * GROUP), F8),
        ],
        compiler_params=pltpu.CompilerParams(vmem_limit_bytes=36 * 2**20),
        name="deposit",
    )(rows)


def join_rows(own, bottom, top):
    return jnp.concatenate([own, jnp.concatenate([bottom, top], axis=0)], axis=0)


def ends(first, second, inside):
    me, count = lax.axis_index("gx"), lax.axis_size("gx")
    bottom, top = side("gx", first, second), side("gx", second, first)
    if inside:
        bottom = jnp.where(me == count - 1, 0.0, bottom)
        top = jnp.where(me == 0, 0.0, top)
    return bottom, top


def strip_lanes(plane, group, lane):
    near = pltpu.roll(plane[:, :128], (group * 16 + 4) % 128, 1)
    far = pltpu.roll(plane[:, 128:], (group * 16 + 8 - 124) % 128, 1)
    at = lane - group * 16
    out = jnp.where((at >= 4) & (at < 8), near, 0.0)
    return jnp.where((at >= 8) & (at < 12), far, out)


def repeat_groups(x):
    for turn in (16, 32, 64):
        x = x + pltpu.roll(x, turn, 1)
    return x


def fill_ring(ref, p):
    for half in range(2):
        ref[half, p, pl.ds(0, 8), :] = ref[half, p, pl.ds(72, 8), :]
        ref[half, p, pl.ds(80, 8), :] = ref[half, p, pl.ds(8, 8), :]


def strips_kernel(state_ref, wet_ref, first_ref, second_ref, out_ref, wets_ref, all_ref):
    planes = state_ref.shape[0]
    lane = iota((72, 128), 1)
    wet = wet_ref[...].astype(F32)
    plane = join_rows(wet, *ends(first_ref[planes], second_ref[planes], True))
    wets_ref[...] = plane
    out_ref[FIELDS] = repeat_groups(strip_lanes(plane, 0, lane))
    for f in range(FIELDS):
        total = None
        for k in range(LEVELS):
            p = f * LEVELS + k
            plane = join_rows(state_ref[p] * wet, *ends(first_ref[p], second_ref[p], True))
            for half in range(2):
                all_ref[half, p, pl.ds(8, 72), :] = plane[:, half * 128:half * 128 + 128]
            fill_ring(all_ref, p)
            piece = strip_lanes(plane, k, lane)
            total = piece if total is None else total + piece
        out_ref[f] = total


def strips(state, wet, first, second):
    planes, rows, cols = state.shape
    return pl.pallas_call(
        strips_kernel,
        out_shape=(
            jax.ShapeDtypeStruct((FIELDS + 1, 72, 128), F32),
            jax.ShapeDtypeStruct((72, cols), F32),
            jax.ShapeDtypeStruct((2, planes, 88, 128), F32),
        ),
        compiler_params=pltpu.CompilerParams(vmem_limit_bytes=16 * 2**20),
        name="strips",
    )(state, wet, first, second)


def forcing_strips_kernel(forcing_ref, first_ref, second_ref, out_ref):
    lane = iota((72, 128), 1)
    total = None
    for f in range(6):
        plane = join_rows(forcing_ref[pl.ds(f * 64, 64), :], *ends(first_ref[f], second_ref[f], False))
        piece = strip_lanes(plane, f, lane)
        total = piece if total is None else total + piece
    out_ref[...] = total


def forcing_strips(forcing, first, second):
    return pl.pallas_call(
        forcing_strips_kernel,
        out_shape=jax.ShapeDtypeStruct((72, 128), F32),
        compiler_params=pltpu.CompilerParams(vmem_limit_bytes=8 * 2**20),
        name="forcing_strips",
    )(forcing, first, second)


def merge(own, first, second):
    gy, count = lax.axis_index("gy"), lax.axis_size("gy")
    slot = iota(own.shape, 1) & 15
    left = jnp.where(gy == 0, 0.0, side("gy", second, first))
    right = jnp.where(gy == count - 1, 0.0, side("gy", first, second))
    out = jnp.where(slot < 4, pltpu.roll(left, 120, 1), own)
    return jnp.where(slot >= 12, pltpu.roll(right, 8, 1), out)


def fill_strip(ref, f):
    ref[f, pl.ds(0, 8), :] = ref[f, pl.ds(72, 8), :]
    ref[f, pl.ds(80, 8), :] = ref[f, pl.ds(8, 8), :]


def merge_strips(own_ref, first_ref, second_ref, strip, swet):
    for f in range(FIELDS):
        strip[f, pl.ds(8, 72), :] = merge(own_ref[f], first_ref[f], second_ref[f])
        fill_strip(strip, f)
    swet[...] = merge(own_ref[FIELDS], first_ref[FIELDS], second_ref[FIELDS])


def mixing_of(force):
    square = force * force
    return square / (1.0 + square)


def coriolis(y):
    base = (lax.axis_index("gy") * 256).astype(F32)
    total = 256.0 * lax.axis_size("gy")
    return 0.1 * (0.5 + 0.5 * ((base + y.astype(F32)) / total - 0.5))


def main_tiles(src, strip, dst, wets, forc, start, stop, final, after=None, beside=None):
    lane8 = iota((8, 128), 1)
    first, last_lane = lane8 == 0, lane8 == 127
    decay = [math.exp(-k) for k in range(LEVELS)]
    heat = [0.05 * math.exp(-0.5 * k) for k in range(LEVELS)]
    turns = [coriolis(lane8 + 128 * half) for half in range(2)]

    def tile(i, carry):
        r = pl.multiple_of(i * 8, 8)
        if beside is not None:
            beside(r)
        for half in range(2):
            here = pl.ds(half * 128, 128)
            wet = wets[pl.ds(r, 8), here]
            force = [forc[f, pl.ds(r, 8), here] for f in range(6)]
            turn = turns[half]
            edge = [strip[f, pl.ds(r + 8, 8), :] for f in range(FIELDS)]
            center = [src[half, f * LEVELS, pl.ds(r + 8, 8), :] for f in range(FIELDS)]
            below = [None] * FIELDS
            px, py = 0.0, 0.0
            for k in range(LEVELS):
                hu, hv = 0.05 * center[0], 0.05 * center[1]
                from_east, from_west, from_north, from_south = 0.025 - hu, 0.025 + hu, 0.025 - hv, 0.025 + hv
                sides = []
                for f in range(FIELDS):
                    p = f * LEVELS + k
                    c = center[f]
                    other = src[1 - half, p, pl.ds(r + 8, 8), :]
                    east = src[half, p, pl.ds(r + 9, 8), :]
                    west = src[half, p, pl.ds(r + 7, 8), :]
                    if half == 0:
                        outer = pltpu.roll(edge[f], (128 - (k * 16 + 3)) % 128, 1)
                        south = jnp.where(first, outer, pltpu.roll(c, 1, 1))
                        north = pltpu.roll(jnp.where(first, other, c), 127, 1)
                    else:
                        outer = pltpu.roll(edge[f], (127 - (k * 16 + 12)) % 128, 1)
                        south = pltpu.roll(jnp.where(last_lane, other, c), 1, 1)
                        north = jnp.where(last_lane, outer, pltpu.roll(c, 127, 1))
                    sides.append((east, west, north, south))
                (e2, w2, n2, s2), (e3, w3, n3, s3) = sides[2:]
                px = px + ((e3 - e2) - (w3 - w2))
                py = py + ((n3 - n2) - (s3 - s2))
                if k + 1 < LEVELS:
                    upper = [src[half, f * LEVELS + k + 1, pl.ds(r + 8, 8), :] for f in range(FIELDS)]
                    diffusivity = 0.03 + (0.12 * decay[k]) * force[5]
                for f in range(FIELDS):
                    east, west, north, south = sides[f]
                    value = 0.9 * center[f] + (
                        (east * from_east + west * from_west) + (north * from_north + south * from_south)
                    )
                    if below[f] is not None:
                        value = value - below[f]
                    if f == 0:
                        value = value + turn * center[1] - 0.01 * px
                    if f == 1:
                        value = value - turn * center[0] - 0.01 * py
                    if f == 2:
                        value = value + heat[k] * force[3]
                    if k == 0:
                        value = value + 0.1 * force[(0, 1, 2, 4)[f]]
                    if k + 1 < LEVELS:
                        below[f] = diffusivity * (upper[f] - center[f])
                        value = value + below[f]
                    if final:
                        dst[f * LEVELS + k, pl.ds(r, 8), here] = wet * value
                    else:
                        dst[half, f * LEVELS + k, pl.ds(r + 8, 8), :] = wet * value
                if k + 1 < LEVELS:
                    center = upper
        if after is not None:
            after(i, r)
        return carry

    lax.fori_loop(start, stop, tile, 0)


SPLIT = 4


def begin_kernel(va, wets, own_ref, first_ref, second_ref, forcing_ref, vb, strip, swet, forc):
    merge_strips(own_ref, first_ref, second_ref, strip, swet)
    for f in range(6):
        plane = forcing_ref[pl.ds(f * 64, 64), :]
        forc[f, pl.ds(0, 64), :] = mixing_of(plane) if f == 5 else plane
    main_tiles(va, strip, vb, wets, forc, 0, SPLIT, False)


def begin(va, wets, own, first, second, forcing):
    planes = FIELDS * LEVELS
    return pl.pallas_call(
        begin_kernel,
        out_shape=(
            jax.ShapeDtypeStruct((2, planes, 88, 128), F32),
            jax.ShapeDtypeStruct((FIELDS, 88, 128), F32),
            jax.ShapeDtypeStruct((72, 128), F32),
            jax.ShapeDtypeStruct((6, 72, 256), F32),
        ),
        compiler_params=pltpu.CompilerParams(vmem_limit_bytes=16 * 2**20),
        cost_estimate=pl.CostEstimate(flops=4 * 10**6, bytes_accessed=6 * 10**6, transcendentals=0),
        name="begin",
    )(va, wets, own, first, second, forcing)


def go_on_kernel(va, wets, strip, half_done, half_forc, ffirst_ref, fsecond_ref, vb, forc):
    for f in range(6):
        ring = jnp.concatenate(ends(ffirst_ref[f], fsecond_ref[f], False), axis=0)
        forc[f, pl.ds(64, 8), :] = mixing_of(ring) if f == 5 else ring
    main_tiles(va, strip, vb, wets, forc, SPLIT, 9, False)
    for p in range(FIELDS * LEVELS):
        fill_ring(vb, p)


def go_on(va, wets, strip, vb, forc, ffirst, fsecond):
    return pl.pallas_call(
        go_on_kernel,
        out_shape=(jax.ShapeDtypeStruct(vb.shape, F32), jax.ShapeDtypeStruct(forc.shape, F32)),
        input_output_aliases={3: 0, 4: 1},
        compiler_params=pltpu.CompilerParams(vmem_limit_bytes=16 * 2**20),
        cost_estimate=pl.CostEstimate(flops=4 * 10**6, bytes_accessed=6 * 10**6, transcendentals=0),
        name="go_on",
    )(va, wets, strip, vb, forc, ffirst, fsecond)


def ocean_kernel(vb, wets, ta, swet, forc, fown_ref, fsfirst_ref, fssecond_ref,
                 out_hbm, out_ref, out_sems, va, vc, tb, tc, sforc):
    planes = FIELDS * LEVELS
    lane = iota((72, 128), 1)
    fwhole = merge(fown_ref[...], fsfirst_ref[...], fssecond_ref[...])
    for f in range(6):
        one = jnp.where(lane < 16, pltpu.roll(fwhole, (128 - 16 * f) % 128, 1), 0.0)
        one = repeat_groups(one)
        sforc[f] = mixing_of(one) if f == 5 else one
    lane8 = iota((8, 128), 1)
    slot8 = lane8 & 15
    scor = coriolis(jnp.where(slot8 < 8, slot8 - 4, slot8 + 244))
    level8 = (lane8 >> 4).astype(F32)
    fade = jnp.exp(-level8)
    solar = 0.05 * jnp.exp(-0.5 * level8)
    surface = jnp.where(lane8 < 16, 0.1, 0.0)

    def scan_levels(x):
        for turn in (16, 32, 64):
            x = x + jnp.where(lane8 >= turn, pltpu.roll(x, turn, 1), 0.0)
        return x

    def strip_tile(src, dst, r):
        force = [sforc[f, pl.ds(r, 8), :] for f in range(6)]
        center = [src[f, pl.ds(r + 8, 8), :] for f in range(FIELDS)]
        east = [src[f, pl.ds(r + 9, 8), :] for f in range(FIELDS)]
        west = [src[f, pl.ds(r + 7, 8), :] for f in range(FIELDS)]
        north = [pltpu.roll(c, 127, 1) for c in center]
        south = [pltpu.roll(c, 1, 1) for c in center]
        dx = [a - b for a, b in zip(east, west)]
        dy = [a - b for a, b in zip(north, south)]
        px = scan_levels(dx[3] - dx[2])
        py = scan_levels(dy[3] - dy[2])
        diffusivity = jnp.where(lane8 < 112, 0.03 + 0.12 * fade * force[5], 0.0)
        hu, hv = 0.05 * center[0], 0.05 * center[1]
        for f in range(FIELDS):
            value = 0.9 * center[f] + 0.025 * ((east[f] + west[f]) + (north[f] + south[f]))
            value = value - hu * dx[f] - hv * dy[f]
            flow = diffusivity * (pltpu.roll(center[f], 112, 1) - center[f])
            value = value + flow - pltpu.roll(flow, 16, 1)
            if f == 0:
                value = value + scor * center[1] - 0.01 * px
            if f == 1:
                value = value - scor * center[0] - 0.01 * py
            if f == 2:
                value = value + solar * force[3]
            value = value + surface * force[(0, 1, 2, 4)[f]]
            dst[f, pl.ds(r + 8, 8), :] = swet[pl.ds(r, 8), :] * value

    def send(i, r):
        done = pl.ds(r, 8)
        pltpu.make_async_copy(out_ref.at[:, done], out_hbm.at[:, done], out_sems.at[i]).start()

    def step(source, strip, target, later):
        main_tiles(source, strip, target, wets, forc, 0, 9, False, beside=lambda r: strip_tile(strip, later, r))
        for p in range(planes):
            fill_ring(target, p)
        for f in range(FIELDS):
            fill_strip(later, f)

    for i in range(9):
        strip_tile(ta, tb, i * 8)
    for f in range(FIELDS):
        fill_strip(tb, f)
    step(vb, tb, va, tc)
    step(va, tc, vc, tb)
    main_tiles(vc, tb, out_ref, wets, forc, 0, 8, True, send)
    for i in range(8):
        done = pl.ds(i * 8, 8)
        pltpu.make_async_copy(out_ref.at[:, done], out_hbm.at[:, done], out_sems.at[i]).wait()


def ocean(*args):
    planes = FIELDS * LEVELS
    return pl.pallas_call(
        ocean_kernel,
        out_shape=jax.ShapeDtypeStruct((planes, 64, 256), F32),
        out_specs=pl.BlockSpec(memory_space=pltpu.HBM),
        scratch_shapes=[
            pltpu.VMEM((planes, 64, 256), F32),
            pltpu.SemaphoreType.DMA((8,)),
            pltpu.VMEM((2, planes, 88, 128), F32),
            pltpu.VMEM((2, planes, 88, 128), F32),
            pltpu.VMEM((FIELDS, 88, 128), F32),
            pltpu.VMEM((FIELDS, 88, 128), F32),
            pltpu.VMEM((6, 72, 128), F32),
        ],
        compiler_params=pltpu.CompilerParams(vmem_limit_bytes=24 * 2**20),
        name="ocean",
    )(*args)


def swap(first, second, axis):
    n = lax.axis_size(axis)
    pairs = [(i, i ^ 1) for i in range(n)]
    others = [(i, (i + (1 if i % 2 else n - 1)) % n) for i in range(n)]
    return lax.ppermute(first, axis, pairs), lax.ppermute(second, axis, others)


def per_device(fluxes, remap_weights, source_elem, owner_map, target_cell, ocean_state, wet_mask):
    state = ocean_state.reshape(FIELDS * LEVELS, 64, 256)
    payload0, payload1, first, second = remap(fluxes, remap_weights, source_elem, target_cell, state, wet_mask)
    first, second = swap(first, second, "gx")
    sent = pack(payload0, payload1, owner_map)
    sent, first, second = lax.optimization_barrier((sent, first, second))
    rows = lax.all_to_all(sent, ("gx", "gy"), split_axis=0, concat_axis=0, tiled=True)
    own, wets, va = strips(state, wet_mask, first, second)
    sfirst, ssecond = swap(own, own, "gy")
    forcing, ffirst, fsecond = deposit(rows)
    ffirst, fsecond = swap(ffirst, fsecond, "gx")
    vb, strip, swet, forc = begin(va, wets, own, sfirst, ssecond, forcing)
    forcing, vb = lax.optimization_barrier((forcing, vb))
    fown = forcing_strips(forcing, ffirst, fsecond)
    fsfirst, fssecond = swap(fown, fown, "gy")
    vb, forc = go_on(va, wets, strip, vb, forc, ffirst, fsecond)
    out = ocean(vb, wets, strip, swet, forc, fown, fsfirst, fssecond)
    return out.reshape(ocean_state.shape)


def solution(mesh):
    in_specs = (
        P(None, None, ("gx", "gy")),
        P(None, None, ("gx", "gy")),
        P(("gx", "gy")),
        P(None, ("gx", "gy")),
        P(None, ("gx", "gy")),
        P(None, None, "gx", "gy"),
        P("gx", "gy"),
    )
    out_specs = P(None, None, "gx", "gy")
    return jax.shard_map(per_device, mesh=mesh, in_specs=in_specs, out_specs=out_specs, check_vma=False)
```

```python
import math

import jax
import jax.numpy as jnp
from jax import lax
from jax.sharding import PartitionSpec as P
from jax.experimental import pallas as pl
from jax.experimental.pallas import tpu as pltpu
F32, BF16, I32 = jnp.float32, jnp.bfloat16, jnp.int32
FIELDS, LEVELS, HALO, STEPS = 4, 8, 4, 4
GROUP = 64
REST = 4096.0
F8 = jnp.float8_e4m3fn
TIGHT = 66 * 10**6
PACK_GROUP = 16
ROWS_DIMS = (((1,), (1,)), ((), ()))


def iota(shape, dim, dtype=I32):
    return lax.broadcasted_iota(dtype, shape, dim)


def split2(v):
    top = v.astype(BF16).astype(F32)
    return top, v - top


def spread16(row):
    return jnp.broadcast_to(row, (16, row.shape[1])).astype(BF16)


def lines16(count, width):
    steps = iota((16, width), 0).astype(F32)
    return [(steps + 16.0 * i).astype(BF16) for i in range(count)]


def side(axis, even, odd):
    return jnp.where(lax.axis_index(axis) % 2 == 0, even, odd)


def remap_kernel(flux_hbm, weight_hbm, source_hbm, cell_hbm, state_hbm, wet_hbm,
                 payload0, payload1, first_ref, second_ref,
                 flux_ref, weight0_ref, weight1_ref, source_ref, cell_ref, low_ref, high_ref,
                 wet_low, wet_high, gathered0, gathered1, sems):
    nt, nj = cell_ref.shape
    fields, nodes = 6, 16
    planes, rows, _ = state_hbm.shape
    copies = [
        pltpu.make_async_copy(source_hbm, source_ref, sems.at[0]),
        pltpu.make_async_copy(flux_hbm, flux_ref, sems.at[1]),
        pltpu.make_async_copy(weight_hbm.at[:, pl.ds(0, 128)], weight0_ref, sems.at[2]),
        pltpu.make_async_copy(weight_hbm.at[:, pl.ds(128, 128)], weight1_ref, sems.at[3]),
        pltpu.make_async_copy(cell_hbm, cell_ref, sems.at[4]),
        pltpu.make_async_copy(wet_hbm.at[pl.ds(0, 8)], wet_low, sems.at[5]),
        pltpu.make_async_copy(wet_hbm.at[pl.ds(rows - 8, 8)], wet_high, sems.at[6]),
        pltpu.make_async_copy(state_hbm.at[:, pl.ds(0, 8)], low_ref, sems.at[7]),
        pltpu.make_async_copy(state_hbm.at[:, pl.ds(rows - 8, 8)], high_ref, sems.at[8]),
    ]
    for copy in copies:
        copy.start()
    copies[0].wait()
    copies[1].wait()
    flux = flux_ref[...]
    f1 = flux.astype(BF16)
    r1 = flux - f1.astype(F32)
    f2 = r1.astype(BF16)
    f3 = (r1 - f2.astype(F32)).astype(BF16)
    elem_hot = jnp.where(iota((flux.shape[1], nj), 0) == source_ref[...], 1.0, 0.0).astype(BF16)
    g = jnp.dot(f1, elem_hot, preferred_element_type=F32)
    g = g + jnp.dot(f2, elem_hot, preferred_element_type=F32)
    g = g + jnp.dot(f3, elem_hot, preferred_element_type=F32)
    gathered0[...] = g[:, :128]
    gathered1[...] = g[:, 128:]
    for copy in copies[2:]:
        copy.wait()
    halves = ((weight0_ref, gathered0, payload0), (weight1_ref, gathered1, payload1))
    for half, (weight_ref, gathered, payload) in enumerate(halves):
        for f in range(fields):
            acc = None
            for s in range(nodes):
                term = weight_ref[pl.ds(s, nt, stride=nodes), :] * gathered[pl.ds(f * nodes + s, 1), :]
                acc = term if acc is None else acc + term
            payload[pl.ds(f, nt, stride=8), :] = acc
        cells = cell_ref[:, pl.ds(half * 128, 128)]
        payload[pl.ds(6, nt, stride=8), :] = (cells >> 8).astype(F32)
        payload[pl.ds(7, nt, stride=8), :] = (cells & 255).astype(F32)
    wl = wet_low[...].astype(F32)[:HALO]
    wh = wet_high[...].astype(F32)[8 - HALO:]
    for p in range(planes):
        lo = low_ref[p][:HALO] * wl
        hi = high_ref[p][8 - HALO:] * wh
        first_ref[p] = side("gx", hi, lo)
        second_ref[p] = side("gx", lo, hi)
    first_ref[planes] = side("gx", wh, wl)
    second_ref[planes] = side("gx", wl, wh)


def remap(fluxes, weights, source, cell, state, wet):
    nf, nn, ne = fluxes.shape
    nt, _, nj = weights.shape
    planes, rows, cols = state.shape
    pay = jax.ShapeDtypeStruct((nt * 8, 128), F32)
    edge = jax.ShapeDtypeStruct((planes + 1, HALO, cols), F32)
    return pl.pallas_call(
        remap_kernel,
        out_shape=(pay, pay, edge, edge),
        in_specs=[pl.BlockSpec(memory_space=pltpu.HBM)] * 6,
        scratch_shapes=[
            pltpu.VMEM((nf * nn, ne), F32),
            pltpu.VMEM((nt * nn, 128), F32),
            pltpu.VMEM((nt * nn, 128), F32),
            pltpu.VMEM((1, nj), I32),
            pltpu.VMEM((nt, nj), I32),
            pltpu.VMEM((planes, 8, cols), F32),
            pltpu.VMEM((planes, 8, cols), F32),
            pltpu.VMEM((8, cols), I32),
            pltpu.VMEM((8, cols), I32),
            pltpu.VMEM((nf * nn, 128), F32),
            pltpu.VMEM((nf * nn, 128), F32),
            pltpu.SemaphoreType.DMA((9,)),
        ],
        compiler_params=pltpu.CompilerParams(vmem_limit_bytes=TIGHT),
        name="remap",
    )(fluxes.reshape(nf * nn, ne), weights.reshape(nt * nn, nj), source.reshape(1, nj), cell, state, wet)


def pack_kernel(payload0, payload1, owner_ref, out_hbm, out_ref, out_sems, hots, place, sorted_rows, left, right, left8, right8, marks, marks_s, sem):
    nt, nj = owner_ref.shape
    owners = out_ref.shape[0]
    owner_iota = iota((owners, nj), 0)
    one, zero = jnp.ones((16, nj), BF16), jnp.zeros((16, nj), BF16)
    lines = lines16(nj // 16, nj)
    totals = [zero] * (owners // 16)
    for t in range(nt):
        o16 = spread16(owner_ref[pl.ds(t, 1), :].astype(F32))
        for i in range(owners // 16):
            hot = jnp.where(o16 == lines[i], one, zero)
            hots[pl.ds(t * owners + i * 16, 16), :] = hot
            totals[i] = totals[i] + hot
    total = jnp.concatenate(totals, axis=0)
    ones = jnp.ones((nj, owners), BF16)
    tot_col = jnp.dot(total, ones, preferred_element_type=F32)
    tot_row = lax.dot_general(jnp.ones((8, nj), BF16), total, ROWS_DIMS, preferred_element_type=F32)
    a = iota((owners, owners), 0)
    b = iota((owners, owners), 1)
    before = jnp.where(b < a, 1.0, 0.0).astype(BF16)
    after = jnp.where(a < b, 1.0, 0.0).astype(BF16)
    base = jnp.dot(before, tot_col.astype(BF16), preferred_element_type=F32)
    start_row = jnp.dot(tot_row.astype(BF16), after, preferred_element_type=F32)
    marks[pl.ds(0, 8), :] = start_row.astype(I32)
    marks[pl.ds(8, 8), :] = tot_row.astype(I32)
    copy = pltpu.make_async_copy(marks, marks_s, sem)
    copy.start()
    ua = iota((nj, nj + owners), 0)
    ub = iota((nj, nj + owners), 1)
    upper = jnp.where((ua < ub) | (ub >= nj), 1.0, 0.0).astype(BF16)
    for t in range(nt):
        hot = hots[pl.ds(t * owners, owners), :]
        r = jnp.dot(hot, upper, preferred_element_type=F32)
        both = jnp.concatenate([base] * (nj // owners), axis=1)
        mine = jnp.where(owner_iota == owner_ref[pl.ds(t, 1), :], r[:, :nj] + both, 0.0)
        place[pl.ds(t, 1), :] = jnp.sum(mine, axis=0, keepdims=True)
        base = base + r[:, nj:]
    pairs = [(2 * i + (iota((16, nj), 0) >> 3)).astype(F32).astype(BF16) for i in range(16)]
    acc = None
    for c in range(nt // PACK_GROUP):
        for u in range(PACK_GROUP):
            t = c * PACK_GROUP + u
            at = pl.ds(u * nj, nj)
            pos = place[pl.ds(t, 1), :].astype(I32)
            high16 = spread16((pos >> 8).astype(F32))
            low16 = spread16((pos & 255).astype(F32))
            top, rest = split2(jnp.concatenate([payload0[pl.ds(t * 8, 8), :], payload1[pl.ds(t * 8, 8), :]], axis=1))
            words = jnp.concatenate([top, top], axis=0).astype(BF16)
            small = (REST * jnp.concatenate([rest, rest], axis=0)).astype(BF16)
            for h in range(8):
                hots_here = [high16 == pairs[2 * h + i] for i in range(2)]
                for i in range(2):
                    left[pl.ds((2 * h + i) * 16, 16), at] = jnp.where(hots_here[i], words, zero)
                left8[pl.ds(h * 32, 32), at] = jnp.concatenate(
                    [jnp.where(hots_here[i], small, zero) for i in range(2)], axis=0
                ).astype(F8)
            for h in range(nj // 32):
                hots_here = [jnp.where(low16 == lines[2 * h + i], one, zero) for i in range(2)]
                for i in range(2):
                    right[pl.ds((2 * h + i) * 16, 16), at] = hots_here[i]
                right8[pl.ds(h * 32, 32), at] = jnp.concatenate(hots_here, axis=0).astype(F8)
        part = lax.dot_general(left[...], right[...], ROWS_DIMS, preferred_element_type=F32)
        small = lax.dot_general(left8[...], right8[...], ROWS_DIMS, preferred_element_type=F32)
        part = part + (1.0 / REST) * small
        acc = part if acc is None else acc + part
    for h in range(32):
        sorted_rows[2 * h] = acc[h * 8:h * 8 + 8, :128]
        sorted_rows[2 * h + 1] = acc[h * 8:h * 8 + 8, 128:]
    zero = jnp.zeros((8, 128), F32)
    sorted_rows[64] = zero
    sorted_rows[65] = zero
    sorted_rows[66] = zero
    copy.wait()
    lane = iota((8, 128), 1)

    def expand(o, carry):
        start = marks_s[0, o]
        count = marks_s[8, o]
        blk = start >> 7
        off = start & 127
        turn = (128 - off) & 127
        v0 = pltpu.roll(sorted_rows[blk], turn, 1)
        v1 = pltpu.roll(sorted_rows[blk + 1], turn, 1)
        v2 = pltpu.roll(sorted_rows[blk + 2], turn, 1)
        keep = lane < 128 - off
        out_ref[o, pl.ds(0, 8), :] = jnp.where(lane < count, jnp.where(keep, v0, v1), 0.0)
        out_ref[o, pl.ds(8, 8), :] = jnp.where(lane < count - 128, jnp.where(keep, v1, v2), 0.0)
        return carry

    pieces = [pl.ds(i * 16, 16) for i in range(owners // 16)]
    sends = [pltpu.make_async_copy(out_ref.at[at], out_hbm.at[at], out_sems.at[i]) for i, at in enumerate(pieces)]
    for i, send in enumerate(sends):
        lax.fori_loop(i * 16, i * 16 + 16, expand, 0, unroll=16)
        send.start()
    for send in sends:
        send.wait()


def pack(payload0, payload1, owner):
    nt, nj = owner.shape
    owners = 128
    return pl.pallas_call(
        pack_kernel,
        out_shape=jax.ShapeDtypeStruct((owners, 16, 128), F32),
        out_specs=pl.BlockSpec(memory_space=pltpu.HBM),
        scratch_shapes=[
            pltpu.VMEM((owners, 16, 128), F32),
            pltpu.SemaphoreType.DMA((owners // 16,)),
            pltpu.VMEM((nt * owners, nj), BF16),
            pltpu.VMEM((nt, nj), F32),
            pltpu.VMEM((67, 8, 128), F32),
            pltpu.VMEM((256, PACK_GROUP * nj), BF16),
            pltpu.VMEM((256, PACK_GROUP * nj), BF16),
            pltpu.VMEM((256, PACK_GROUP * nj), F8),
            pltpu.VMEM((256, PACK_GROUP * nj), F8),
            pltpu.VMEM((16, 128), I32),
            pltpu.SMEM((16, 128), I32),
            pltpu.SemaphoreType.DMA,
        ],
        compiler_params=pltpu.CompilerParams(vmem_limit_bytes=TIGHT),
        name="pack",
    )(payload0, payload1, owner)


def deposit_kernel(rows_ref, out_ref, first_ref, second_ref, left, right, left8, right8):
    senders = rows_ref.shape[0]
    fields = 6
    group = GROUP
    one, zero = jnp.ones((16, 256), BF16), jnp.zeros((16, 256), BF16)
    lines = lines16(16, 256)
    for c in range(senders // group):
        for u in range(group):
            d = c * group + u
            tile = jnp.concatenate([rows_ref[d, pl.ds(0, 8), :], rows_ref[d, pl.ds(8, 8), :]], axis=1)
            x16 = spread16(tile[6:7])
            y16 = spread16(tile[7:8])
            top, rest = split2(tile)
            rest = REST * rest
            at = pl.ds(u * 256, 256)
            hots = [jnp.where(x16 == lines[i], one, zero) for i in range(4)]
            for f in range(fields):
                v16 = spread16(top[f:f + 1])
                r16 = spread16(rest[f:f + 1])
                for i in range(4):
                    left[pl.ds(f * 64 + i * 16, 16), at] = hots[i] * v16
                for i in range(2):
                    pair = jnp.concatenate([hots[2 * i] * r16, hots[2 * i + 1] * r16], axis=0)
                    left8[pl.ds(f * 64 + i * 32, 32), at] = pair.astype(F8)
            for i in range(8):
                pair = [jnp.where(y16 == lines[2 * i + j], one, zero) for j in range(2)]
                for j in range(2):
                    right[pl.ds((2 * i + j) * 16, 16), at] = pair[j]
                right8[pl.ds(i * 32, 32), at] = jnp.concatenate(pair, axis=0).astype(F8)
        part = lax.dot_general(left[...], right[...], ROWS_DIMS, preferred_element_type=F32)
        small = lax.dot_general(left8[...], right8[...], ROWS_DIMS, preferred_element_type=F32)
        part = part + (1.0 / REST) * small
        out_ref[...] = part if c == 0 else out_ref[...] + part
    for f in range(fields):
        low = out_ref[pl.ds(f * 64, 8), :][:HALO]
        high = out_ref[pl.ds(f * 64 + 56, 8), :][8 - HALO:]
        first_ref[f] = side("gx", high, low)
        second_ref[f] = side("gx", low, high)


def deposit(rows):
    return pl.pallas_call(
        deposit_kernel,
        out_shape=(
            jax.ShapeDtypeStruct((6 * 64, 256), F32),
            jax.ShapeDtypeStruct((6, HALO, 256), F32),
            jax.ShapeDtypeStruct((6, HALO, 256), F32),
        ),
        scratch_shapes=[
            pltpu.VMEM((384, 256 * GROUP), BF16),
            pltpu.VMEM((256, 256 * GROUP), BF16),
            pltpu.VMEM((384, 256 * GROUP), F8),
            pltpu.VMEM((256, 256 * GROUP), F8),
        ],
        compiler_params=pltpu.CompilerParams(vmem_limit_bytes=36 * 2**20),
        name="deposit",
    )(rows)


def join_rows(own, bottom, top):
    return jnp.concatenate([own, jnp.concatenate([bottom, top], axis=0)], axis=0)


def ends(first, second, inside):
    me, count = lax.axis_index("gx"), lax.axis_size("gx")
    bottom, top = side("gx", first, second), side("gx", second, first)
    if inside:
        bottom = jnp.where(me == count - 1, 0.0, bottom)
        top = jnp.where(me == 0, 0.0, top)
    return bottom, top


def strip_lanes(plane, group, lane):
    near = pltpu.roll(plane[:, :128], (group * 16 + 4) % 128, 1)
    far = pltpu.roll(plane[:, 128:], (group * 16 + 8 - 124) % 128, 1)
    at = lane - group * 16
    out = jnp.where((at >= 4) & (at < 8), near, 0.0)
    return jnp.where((at >= 8) & (at < 12), far, out)


def repeat_groups(x):
    for turn in (16, 32, 64):
        x = x + pltpu.roll(x, turn, 1)
    return x


def fill_ring(ref, p):
    for half in range(2):
        ref[half, p, pl.ds(0, 8), :] = ref[half, p, pl.ds(72, 8), :]
        ref[half, p, pl.ds(80, 8), :] = ref[half, p, pl.ds(8, 8), :]


def strips_kernel(state_ref, wet_ref, first_ref, second_ref, out_ref, wets_ref, all_ref):
    planes = state_ref.shape[0]
    lane = iota((72, 128), 1)
    wet = wet_ref[...].astype(F32)
    plane = join_rows(wet, *ends(first_ref[planes], second_ref[planes], True))
    wets_ref[...] = plane
    out_ref[FIELDS] = repeat_groups(strip_lanes(plane, 0, lane))
    for f in range(FIELDS):
        total = None
        for k in range(LEVELS):
            p = f * LEVELS + k
            plane = join_rows(state_ref[p] * wet, *ends(first_ref[p], second_ref[p], True))
            for half in range(2):
                all_ref[half, p, pl.ds(8, 72), :] = plane[:, half * 128:half * 128 + 128]
            fill_ring(all_ref, p)
            piece = strip_lanes(plane, k, lane)
            total = piece if total is None else total + piece
        out_ref[f] = total


def strips(state, wet, first, second):
    planes, rows, cols = state.shape
    return pl.pallas_call(
        strips_kernel,
        out_shape=(
            jax.ShapeDtypeStruct((FIELDS + 1, 72, 128), F32),
            jax.ShapeDtypeStruct((72, cols), F32),
            jax.ShapeDtypeStruct((2, planes, 88, 128), F32),
        ),
        compiler_params=pltpu.CompilerParams(vmem_limit_bytes=16 * 2**20),
        name="strips",
    )(state, wet, first, second)


def forcing_strips_kernel(forcing_ref, first_ref, second_ref, out_ref):
    lane = iota((72, 128), 1)
    total = None
    for f in range(6):
        plane = join_rows(forcing_ref[pl.ds(f * 64, 64), :], *ends(first_ref[f], second_ref[f], False))
        piece = strip_lanes(plane, f, lane)
        total = piece if total is None else total + piece
    out_ref[...] = total


def forcing_strips(forcing, first, second):
    return pl.pallas_call(
        forcing_strips_kernel,
        out_shape=jax.ShapeDtypeStruct((72, 128), F32),
        compiler_params=pltpu.CompilerParams(vmem_limit_bytes=8 * 2**20),
        name="forcing_strips",
    )(forcing, first, second)


def merge(own, first, second):
    gy, count = lax.axis_index("gy"), lax.axis_size("gy")
    slot = iota(own.shape, 1) & 15
    left = jnp.where(gy == 0, 0.0, side("gy", second, first))
    right = jnp.where(gy == count - 1, 0.0, side("gy", first, second))
    out = jnp.where(slot < 4, pltpu.roll(left, 120, 1), own)
    return jnp.where(slot >= 12, pltpu.roll(right, 8, 1), out)


def fill_strip(ref, f):
    ref[f, pl.ds(0, 8), :] = ref[f, pl.ds(72, 8), :]
    ref[f, pl.ds(80, 8), :] = ref[f, pl.ds(8, 8), :]


def merge_strips(own_ref, first_ref, second_ref, strip, swet):
    for f in range(FIELDS):
        strip[f, pl.ds(8, 72), :] = merge(own_ref[f], first_ref[f], second_ref[f])
        fill_strip(strip, f)
    swet[...] = merge(own_ref[FIELDS], first_ref[FIELDS], second_ref[FIELDS])


def mixing_of(force):
    square = force * force
    return square / (1.0 + square)


def coriolis(y):
    base = (lax.axis_index("gy") * 256).astype(F32)
    total = 256.0 * lax.axis_size("gy")
    return 0.1 * (0.5 + 0.5 * ((base + y.astype(F32)) / total - 0.5))


def main_tiles(src, strip, dst, wets, forc, start, stop, final, after=None, beside=None):
    lane8 = iota((8, 128), 1)
    first, last_lane = lane8 == 0, lane8 == 127
    decay = [math.exp(-k) for k in range(LEVELS)]
    heat = [0.05 * math.exp(-0.5 * k) for k in range(LEVELS)]
    turns = [coriolis(lane8 + 128 * half) for half in range(2)]

    def tile(i, carry):
        r = pl.multiple_of(i * 8, 8)
        if beside is not None:
            beside(r)
        for half in range(2):
            here = pl.ds(half * 128, 128)
            wet = wets[pl.ds(r, 8), here]
            force = [forc[f, pl.ds(r, 8), here] for f in range(6)]
            turn = turns[half]
            edge = [strip[f, pl.ds(r + 8, 8), :] for f in range(FIELDS)]
            center = [src[half, f * LEVELS, pl.ds(r + 8, 8), :] for f in range(FIELDS)]
            below = [None] * FIELDS
            px, py = 0.0, 0.0
            for k in range(LEVELS):
                hu, hv = 0.05 * center[0], 0.05 * center[1]
                from_east, from_west, from_north, from_south = 0.025 - hu, 0.025 + hu, 0.025 - hv, 0.025 + hv
                sides = []
                for f in range(FIELDS):
                    p = f * LEVELS + k
                    c = center[f]
                    other = src[1 - half, p, pl.ds(r + 8, 8), :]
                    east = src[half, p, pl.ds(r + 9, 8), :]
                    west = src[half, p, pl.ds(r + 7, 8), :]
                    if half == 0:
                        outer = pltpu.roll(edge[f], (128 - (k * 16 + 3)) % 128, 1)
                        south = jnp.where(first, outer, pltpu.roll(c, 1, 1))
                        north = pltpu.roll(jnp.where(first, other, c), 127, 1)
                    else:
                        outer = pltpu.roll(edge[f], (127 - (k * 16 + 12)) % 128, 1)
                        south = pltpu.roll(jnp.where(last_lane, other, c), 1, 1)
                        north = jnp.where(last_lane, outer, pltpu.roll(c, 127, 1))
                    sides.append((east, west, north, south))
                (e2, w2, n2, s2), (e3, w3, n3, s3) = sides[2:]
                px = px + ((e3 - e2) - (w3 - w2))
                py = py + ((n3 - n2) - (s3 - s2))
                if k + 1 < LEVELS:
                    upper = [src[half, f * LEVELS + k + 1, pl.ds(r + 8, 8), :] for f in range(FIELDS)]
                    diffusivity = 0.03 + (0.12 * decay[k]) * force[5]
                for f in range(FIELDS):
                    east, west, north, south = sides[f]
                    value = 0.9 * center[f] + (
                        (east * from_east + west * from_west) + (north * from_north + south * from_south)
                    )
                    if below[f] is not None:
                        value = value - below[f]
                    if f == 0:
                        value = value + turn * center[1] - 0.01 * px
                    if f == 1:
                        value = value - turn * center[0] - 0.01 * py
                    if f == 2:
                        value = value + heat[k] * force[3]
                    if k == 0:
                        value = value + 0.1 * force[(0, 1, 2, 4)[f]]
                    if k + 1 < LEVELS:
                        below[f] = diffusivity * (upper[f] - center[f])
                        value = value + below[f]
                    if final:
                        dst[f * LEVELS + k, pl.ds(r, 8), here] = wet * value
                    else:
                        dst[half, f * LEVELS + k, pl.ds(r + 8, 8), :] = wet * value
                if k + 1 < LEVELS:
                    center = upper
        if after is not None:
            after(i, r)
        return carry

    lax.fori_loop(start, stop, tile, 0)


SPLIT = 4


def begin_kernel(va, wets, own_ref, first_ref, second_ref, forcing_ref, vb, strip, swet, forc):
    merge_strips(own_ref, first_ref, second_ref, strip, swet)
    for f in range(6):
        plane = forcing_ref[pl.ds(f * 64, 64), :]
        forc[f, pl.ds(0, 64), :] = mixing_of(plane) if f == 5 else plane
    main_tiles(va, strip, vb, wets, forc, 0, SPLIT, False)


def begin(va, wets, own, first, second, forcing):
    planes = FIELDS * LEVELS
    return pl.pallas_call(
        begin_kernel,
        out_shape=(
            jax.ShapeDtypeStruct((2, planes, 88, 128), F32),
            jax.ShapeDtypeStruct((FIELDS, 88, 128), F32),
            jax.ShapeDtypeStruct((72, 128), F32),
            jax.ShapeDtypeStruct((6, 72, 256), F32),
        ),
        compiler_params=pltpu.CompilerParams(vmem_limit_bytes=16 * 2**20),
        cost_estimate=pl.CostEstimate(flops=4 * 10**6, bytes_accessed=6 * 10**6, transcendentals=0),
        name="begin",
    )(va, wets, own, first, second, forcing)


def go_on_kernel(va, wets, strip, half_done, half_forc, ffirst_ref, fsecond_ref, vb, forc):
    for f in range(6):
        ring = jnp.concatenate(ends(ffirst_ref[f], fsecond_ref[f], False), axis=0)
        forc[f, pl.ds(64, 8), :] = mixing_of(ring) if f == 5 else ring
    main_tiles(va, strip, vb, wets, forc, SPLIT, 9, False)
    for p in range(FIELDS * LEVELS):
        fill_ring(vb, p)


def go_on(va, wets, strip, vb, forc, ffirst, fsecond):
    return pl.pallas_call(
        go_on_kernel,
        out_shape=(jax.ShapeDtypeStruct(vb.shape, F32), jax.ShapeDtypeStruct(forc.shape, F32)),
        input_output_aliases={3: 0, 4: 1},
        compiler_params=pltpu.CompilerParams(vmem_limit_bytes=16 * 2**20),
        cost_estimate=pl.CostEstimate(flops=4 * 10**6, bytes_accessed=6 * 10**6, transcendentals=0),
        name="go_on",
    )(va, wets, strip, vb, forc, ffirst, fsecond)


def ocean_kernel(vb, wets, ta, swet, forc, fown_ref, fsfirst_ref, fssecond_ref,
                 out_hbm, out_ref, out_sems, va, vc, tb, tc, sforc):
    planes = FIELDS * LEVELS
    lane = iota((72, 128), 1)
    fwhole = merge(fown_ref[...], fsfirst_ref[...], fssecond_ref[...])
    for f in range(6):
        one = jnp.where(lane < 16, pltpu.roll(fwhole, (128 - 16 * f) % 128, 1), 0.0)
        one = repeat_groups(one)
        sforc[f] = mixing_of(one) if f == 5 else one
    lane8 = iota((8, 128), 1)
    slot8 = lane8 & 15
    scor = coriolis(jnp.where(slot8 < 8, slot8 - 4, slot8 + 244))
    level8 = (lane8 >> 4).astype(F32)
    fade = jnp.exp(-level8)
    solar = 0.05 * jnp.exp(-0.5 * level8)
    surface = jnp.where(lane8 < 16, 0.1, 0.0)

    def scan_levels(x):
        for turn in (16, 32, 64):
            x = x + jnp.where(lane8 >= turn, pltpu.roll(x, turn, 1), 0.0)
        return x

    def strip_tile(src, dst, r):
        force = [sforc[f, pl.ds(r, 8), :] for f in range(6)]
        center = [src[f, pl.ds(r + 8, 8), :] for f in range(FIELDS)]
        east = [src[f, pl.ds(r + 9, 8), :] for f in range(FIELDS)]
        west = [src[f, pl.ds(r + 7, 8), :] for f in range(FIELDS)]
        north = [pltpu.roll(c, 127, 1) for c in center]
        south = [pltpu.roll(c, 1, 1) for c in center]
        dx = [a - b for a, b in zip(east, west)]
        dy = [a - b for a, b in zip(north, south)]
        px = scan_levels(dx[3] - dx[2])
        py = scan_levels(dy[3] - dy[2])
        diffusivity = jnp.where(lane8 < 112, 0.03 + 0.12 * fade * force[5], 0.0)
        hu, hv = 0.05 * center[0], 0.05 * center[1]
        for f in range(FIELDS):
            value = 0.9 * center[f] + 0.025 * ((east[f] + west[f]) + (north[f] + south[f]))
            value = value - hu * dx[f] - hv * dy[f]
            flow = diffusivity * (pltpu.roll(center[f], 112, 1) - center[f])
            value = value + flow - pltpu.roll(flow, 16, 1)
            if f == 0:
                value = value + scor * center[1] - 0.01 * px
            if f == 1:
                value = value - scor * center[0] - 0.01 * py
            if f == 2:
                value = value + solar * force[3]
            value = value + surface * force[(0, 1, 2, 4)[f]]
            dst[f, pl.ds(r + 8, 8), :] = swet[pl.ds(r, 8), :] * value

    def send(i, r):
        done = pl.ds(r, 8)
        pltpu.make_async_copy(out_ref.at[:, done], out_hbm.at[:, done], out_sems.at[i]).start()

    def step(source, strip, target, later):
        main_tiles(source, strip, target, wets, forc, 0, 9, False, beside=lambda r: strip_tile(strip, later, r))
        for p in range(planes):
            fill_ring(target, p)
        for f in range(FIELDS):
            fill_strip(later, f)

    for i in range(9):
        strip_tile(ta, tb, i * 8)
    for f in range(FIELDS):
        fill_strip(tb, f)
    step(vb, tb, va, tc)
    step(va, tc, vc, tb)
    main_tiles(vc, tb, out_ref, wets, forc, 0, 8, True, send)
    for i in range(8):
        done = pl.ds(i * 8, 8)
        pltpu.make_async_copy(out_ref.at[:, done], out_hbm.at[:, done], out_sems.at[i]).wait()


def ocean(*args):
    planes = FIELDS * LEVELS
    return pl.pallas_call(
        ocean_kernel,
        out_shape=jax.ShapeDtypeStruct((planes, 64, 256), F32),
        out_specs=pl.BlockSpec(memory_space=pltpu.HBM),
        scratch_shapes=[
            pltpu.VMEM((planes, 64, 256), F32),
            pltpu.SemaphoreType.DMA((8,)),
            pltpu.VMEM((2, planes, 88, 128), F32),
            pltpu.VMEM((2, planes, 88, 128), F32),
            pltpu.VMEM((FIELDS, 88, 128), F32),
            pltpu.VMEM((FIELDS, 88, 128), F32),
            pltpu.VMEM((6, 72, 128), F32),
        ],
        compiler_params=pltpu.CompilerParams(vmem_limit_bytes=24 * 2**20),
        name="ocean",
    )(*args)


def swap(first, second, axis):
    n = lax.axis_size(axis)
    pairs = [(i, i ^ 1) for i in range(n)]
    others = [(i, (i + (1 if i % 2 else n - 1)) % n) for i in range(n)]
    return lax.ppermute(first, axis, pairs), lax.ppermute(second, axis, others)


def per_device(fluxes, remap_weights, source_elem, owner_map, target_cell, ocean_state, wet_mask):
    state = ocean_state.reshape(FIELDS * LEVELS, 64, 256)
    payload0, payload1, first, second = remap(fluxes, remap_weights, source_elem, target_cell, state, wet_mask)
    first, second = swap(first, second, "gx")
    sent = pack(payload0, payload1, owner_map)
    sent, first, second = lax.optimization_barrier((sent, first, second))
    rows = lax.all_to_all(sent, ("gx", "gy"), split_axis=0, concat_axis=0, tiled=True)
    own, wets, va = strips(state, wet_mask, first, second)
    sfirst, ssecond = swap(own, own, "gy")
    forcing, ffirst, fsecond = deposit(rows)
    ffirst, fsecond = swap(ffirst, fsecond, "gx")
    vb, strip, swet, forc = begin(va, wets, own, sfirst, ssecond, forcing)
    forcing, vb = lax.optimization_barrier((forcing, vb))
    fown = forcing_strips(forcing, ffirst, fsecond)
    fsfirst, fssecond = swap(fown, fown, "gy")
    vb, forc = go_on(va, wets, strip, vb, forc, ffirst, fsecond)
    out = ocean(vb, wets, strip, swet, forc, fown, fsfirst, fssecond)
    return out.reshape(ocean_state.shape)


def solution(mesh):
    in_specs = (
        P(None, None, ("gx", "gy")),
        P(None, None, ("gx", "gy")),
        P(("gx", "gy")),
        P(None, ("gx", "gy")),
        P(None, ("gx", "gy")),
        P(None, None, "gx", "gy"),
        P("gx", "gy"),
    )
    out_specs = P(None, None, "gx", "gy")
    return jax.shard_map(per_device, mesh=mesh, in_specs=in_specs, out_specs=out_specs, check_vma=False)
```
